32 devices in a mesh: wide: 8 (over z, x), narrow: 4 (over y, core).
Axes of the slice: x: 2, y: 2, z: 4, core: 2. Of those that a mesh axis runs over, the one named last changes fastest.
Arguments:
- atmos_state: bfloat16 [96, 256, 512], P('narrow', 'wide'), may hold values from -6 to 6
- ocean_state: bfloat16 [96, 256, 512], P('narrow', 'wide'), may hold values from -6 to 6
- wet_mask: int32 [96, 256], P('narrow', 'wide'), may hold values 0 or 1
- atmos_kernel: float32 [7, 7, 512], replicated, may hold values from -0.875 to 0.875
- atmos_gain: float32 [512], replicated, may hold values from 0.1 to 1.9
- atmos_inner: bfloat16 [512, 2048], replicated, may hold values from -0.25 to 0.25
- atmos_outer: bfloat16 [2048, 512], replicated, may hold values from -0.125 to 0.125
- ocean_kernel: float32 [7, 7, 512], replicated, may hold values from -0.875 to 0.875
- ocean_gain: float32 [512], replicated, may hold values from 0.1 to 1.9
- ocean_inner: bfloat16 [512, 2048], replicated, may hold values from -0.25 to 0.25
- ocean_outer: bfloat16 [2048, 512], replicated, may hold values from -0.125 to 0.125
- flux_head: bfloat16 [512, 8], replicated, may hold values from -0.25 to 0.25
- flux_lift: bfloat16 [8, 512], replicated, may hold values from -2 to 2
- surface_head: bfloat16 [512, 8], replicated, may hold values from -0.25 to 0.25
- surface_lift: bfloat16 [8, 512], replicated, may hold values from -2 to 2
- flux_source: int32 [4, 8, 48], P('narrow', 'wide'), may hold values from 0 to 71
- flux_target: int32 [4, 8, 48], P('narrow', 'wide'), may hold values from 0 to 5
- flux_weight: float32 [4, 8, 48], P('narrow', 'wide'), may hold values from 0.2 to 1
- surface_source: int32 [4, 8, 48], P('narrow', 'wide'), may hold values from 0 to 71
- surface_target: int32 [4, 8, 48], P('narrow', 'wide'), may hold values from 0 to 5
- surface_weight: float32 [4, 8, 48], P('narrow', 'wide'), may hold values from 0.2 to 1
- atmos_cotangent: bfloat16 [96, 256, 512], P('narrow', 'wide'), may hold values from -6 to 6
- ocean_cotangent: bfloat16 [96, 256, 512], P('narrow', 'wide'), may hold values from -6 to 6
Outputs:
- atmos_next: bfloat16 [96, 256, 512], P('narrow', 'wide')
- ocean_next: bfloat16 [96, 256, 512], P('narrow', 'wide')
- atmos_state_grad: bfloat16 [96, 256, 512], P('narrow', 'wide')
- ocean_state_grad: bfloat16 [96, 256, 512], P('narrow', 'wide')
- atmos_inner_grad: float32 [512, 2048], P(('wide', 'narrow'))
- atmos_outer_grad: float32 [2048, 512], P(('wide', 'narrow'))
- atmos_kernel_grad: float32 [7, 7, 512], replicated
- ocean_inner_grad: float32 [512, 2048], P(('wide', 'narrow'))
- ocean_outer_grad: float32 [2048, 512], P(('wide', 'narrow'))
- ocean_kernel_grad: float32 [7, 7, 512], replicated
The draws below stay inside these ranges and needn't reach their ends.
Inputs may be any that keep to these rules, and one draw needn't show every extreme that they name: `flux_source`: A value (o * 4 + m) * 6 + s names block s of the tile in latitude row m and longitude column w + o - 1, taken periodically, for a target tile in longitude column w. `flux_target`: block of the target tile that receives the entry. `surface_source`: A value (o * 4 + m) * 6 + s names block s of the tile in latitude row m and longitude column w + o - 1, taken periodically, for a target tile in longitude column w. `surface_target`: block of the target tile that receives the entry. `wet_mask`: 1 marks a sea cell, 0 a land cell.
All inputs are finite; a program needn't handle non-finite values. No bound on the sum of `wet_mask` on one device may be relied on, other than what follows from the above.
Results may differ from the reference program's by a relative error of at most 0.015.
Values may be sent and summed in bfloat16 or wider, within the bound.
No kernel may reach another device: no remote copies, remote signals or barrier semaphores. Data moves between devices by JAX's collectives and lax.ppermute only.
A program may use at most 192 MiB of HBM per device.

```python
import jax
import jax.numpy as jnp
from jax import lax

D = 512
FF = 2048
KERNEL = 7
CPL = 8
ROWS = 24
COLS = 32
LAT_TILES = 4
LON_TILES = 8
LAT = 96
LON = 256
NB = 6
ENT = 48


def with_ends(entries, rng, least, high):
    dims = entries.shape
    place = [jax.random.randint(jax.random.fold_in(rng, axis), (), 0, dims[axis]) for axis in range(len(dims))]
    entries = entries.at[tuple(place)].set(least)
    longest = dims.index(max(dims))
    place[longest] = (place[longest] + 1) % dims[longest]
    return entries.at[tuple(place)].set(high)


def block_scale(stream_key, shape, cuts, low, largest):
    gain, own = 1.0, jax.random.fold_in(stream_key, 6)
    for position, shards_of in cuts:
        draws = jnp.exp(jax.random.uniform(jax.random.fold_in(own, position), (shards_of,), jnp.float32, low / len(cuts), largest / len(cuts)))
        gain = gain * jnp.repeat(draws, shape[position] // shards_of).reshape([-1 if axis == position else 1 for axis in range(len(shape))])
    return gain


def bell_draw(key, dims, deviation, bound, split=(), kind=jnp.bfloat16):
    values = jax.random.normal(key, dims, jnp.float32) * deviation
    if len(split) > 0:
        values = block_scale(key, dims, split, -0.22, 0.18) * values
    return jnp.clip(values, min=-bound, max=bound).astype(kind)


def setup_inputs(seed: int = 0) -> dict:
    key_list = jax.random.split(jax.random.key(seed), 24)
    atmos_state = bell_draw(key_list[0], (LAT, LON, D), 1.0, 6.0, ((0, 4), (1, 8)))
    ocean_state = bell_draw(key_list[1], (LAT, LON, D), 1.0, 6.0, ((0, 4), (1, 8)))
    wet_mask = with_ends((jax.random.randint(key_list[2], (LAT, LON), 0, 4) < 3).astype(jnp.int32), jax.random.fold_in(key_list[2], 1), 0, 1)
    atmos_kernel = bell_draw(key_list[3], (KERNEL, KERNEL, D), (KERNEL * KERNEL) ** -0.5, 0.875, (), jnp.float32)
    atmos_gain = jnp.clip(1.0 + 0.18 * jax.random.normal(key_list[4], (D,), jnp.float32), 0.1, 1.9)
    atmos_inner = bell_draw(key_list[5], (D, FF), D ** -0.5, 0.25)
    atmos_outer = bell_draw(key_list[6], (FF, D), FF ** -0.5, 0.125)
    ocean_kernel = bell_draw(key_list[7], (KERNEL, KERNEL, D), (KERNEL * KERNEL) ** -0.5, 0.875, (), jnp.float32)
    ocean_gain = jnp.clip(1.0 + 0.18 * jax.random.normal(key_list[8], (D,), jnp.float32), 0.1, 1.9)
    ocean_inner = bell_draw(key_list[9], (D, FF), D ** -0.5, 0.25)
    ocean_outer = bell_draw(key_list[10], (FF, D), FF ** -0.5, 0.125)
    flux_head = bell_draw(key_list[11], (D, CPL), D ** -0.5, 0.25)
    flux_lift = bell_draw(key_list[12], (CPL, D), CPL ** -0.5, 2.0)
    surface_head = bell_draw(key_list[13], (D, CPL), D ** -0.5, 0.25)
    surface_lift = bell_draw(key_list[14], (CPL, D), CPL ** -0.5, 2.0)
    flux_source = with_ends(jax.random.randint(key_list[15], (LAT_TILES, LON_TILES, ENT), 0, 3 * LAT_TILES * NB), jax.random.fold_in(key_list[15], 1), 0, (3 * LAT_TILES * NB) - 1).astype(jnp.int32)
    flux_target = with_ends(jax.random.randint(key_list[16], (LAT_TILES, LON_TILES, ENT), 0, NB), jax.random.fold_in(key_list[16], 1), 0, NB - 1).astype(jnp.int32)
    flux_weight = jnp.clip(0.2 + 0.8 * jax.random.uniform(key_list[17], (LAT_TILES, LON_TILES, ENT), jnp.float32) ** block_scale(key_list[17], (LAT_TILES, LON_TILES, ENT), ((0, 4), (1, 8)), -0.2, 0.2), 0.2, 1.0)
    surface_source = with_ends(jax.random.randint(key_list[18], (LAT_TILES, LON_TILES, ENT), 0, 3 * LAT_TILES * NB), jax.random.fold_in(key_list[18], 1), 0, (3 * LAT_TILES * NB) - 1).astype(jnp.int32)
    surface_target = with_ends(jax.random.randint(key_list[19], (LAT_TILES, LON_TILES, ENT), 0, NB), jax.random.fold_in(key_list[19], 1), 0, NB - 1).astype(jnp.int32)
    surface_weight = jnp.clip(0.2 + 0.8 * jax.random.uniform(key_list[20], (LAT_TILES, LON_TILES, ENT), jnp.float32) ** block_scale(key_list[20], (LAT_TILES, LON_TILES, ENT), ((0, 4), (1, 8)), -0.2, 0.2), 0.2, 1.0)
    atmos_cotangent = bell_draw(key_list[21], (LAT, LON, D), 1.0, 6.0, ((0, 4), (1, 8)))
    ocean_cotangent = bell_draw(key_list[22], (LAT, LON, D), 1.0, 6.0, ((0, 4), (1, 8)))
    return {"atmos_state": atmos_state, "ocean_state": ocean_state, "wet_mask": wet_mask, "atmos_kernel": atmos_kernel, "atmos_gain": atmos_gain, "atmos_inner": atmos_inner, "atmos_outer": atmos_outer, "ocean_kernel": ocean_kernel, "ocean_gain": ocean_gain, "ocean_inner": ocean_inner, "ocean_outer": ocean_outer, "flux_head": flux_head, "flux_lift": flux_lift, "surface_head": surface_head, "surface_lift": surface_lift, "flux_source": flux_source, "flux_target": flux_target, "flux_weight": flux_weight, "surface_source": surface_source, "surface_target": surface_target, "surface_weight": surface_weight, "atmos_cotangent": atmos_cotangent, "ocean_cotangent": ocean_cotangent}


norm_eps = 1e-06
grad_scale = 256.0
highest = lax.Precision.HIGHEST

def normal_cdf(values):
    return 0.5 * (1.0 + lax.erf(values * 0.7071067811865476))

def normal_density(values):
    return jnp.exp(-0.5 * values * values) * 0.3989422804014327

def extend(fields, folded):
    margin = KERNEL // 2
    beside = jnp.concatenate([fields[:, -margin:], fields, fields[:, :margin]], axis=1)
    bottom_rows = jnp.zeros_like(beside[:margin])
    if folded:
        top_rows = beside[-margin:][::-1, ::-1]
    else:
        top_rows = jnp.zeros_like(beside[:margin])
    return jnp.concatenate([bottom_rows, beside, top_rows], axis=0)

def apply_kernel(padded, kernel, row_count, col_count):
    running = jnp.zeros((row_count, col_count, kernel.shape[-1]), jnp.float32)
    for row_tap in range(KERNEL):
        for col_tap in range(KERNEL):
            window = padded[row_tap:row_tap + row_count, col_tap:col_tap + col_count]
            running = running + window * kernel[row_tap, col_tap]
    return running

def block_forward(start_field, kernel, norm_gain, inner_weight, outer_weight, folded):
    padded = extend(start_field, folded)
    mixed_taps = apply_kernel(padded, kernel, LAT, LON)
    center = mixed_taps - lax.optimization_barrier(jnp.mean(mixed_taps, axis=-1, keepdims=True))
    inverse = lax.rsqrt(lax.optimization_barrier(jnp.mean(center * center, axis=-1, keepdims=True)) + norm_eps)
    scaled = center * inverse
    normed = (scaled * norm_gain).astype(jnp.bfloat16)

    def mlp_rows(normed_rows):
        before = jnp.dot(normed_rows, inner_weight, preferred_element_type=jnp.float32)
        hidden = (before * normal_cdf(before)).astype(jnp.bfloat16)
        return jnp.dot(hidden, outer_weight, preferred_element_type=jnp.float32)
    branch = lax.map(mlp_rows, normed.reshape(LAT_TILES, ROWS * LON, D)).reshape(LAT, LON, D)
    return (branch, (padded, scaled, inverse, normed))

def block_backward(stored, kernel, norm_gain, inner_weight, outer_weight, incoming, folded):
    padded, scaled, inverse, normed = stored
    rounded = incoming.astype(jnp.bfloat16)

    def grad_rows(partials, pieces):
        inner_sum, outer_sum = partials
        normed_rows, round_rows = pieces
        before = jnp.dot(normed_rows, inner_weight, preferred_element_type=jnp.float32)
        hidden = (before * normal_cdf(before)).astype(jnp.bfloat16)
        d_hidden = jnp.dot(round_rows, outer_weight.T, preferred_element_type=jnp.float32)
        slopes = normal_cdf(before) + before * normal_density(before)
        d_before = (d_hidden * slopes).astype(jnp.bfloat16)
        d_normed = jnp.dot(d_before, inner_weight.T, preferred_element_type=jnp.float32)
        inner_sum = inner_sum + jnp.dot(normed_rows.T, d_before, preferred_element_type=jnp.float32)
        outer_sum = outer_sum + jnp.dot(hidden.T, round_rows, preferred_element_type=jnp.float32)
        return ((inner_sum, outer_sum), d_normed)
    zeros_init = (jnp.zeros((D, FF), jnp.float32), jnp.zeros((FF, D), jnp.float32))
    (inner_sum, outer_sum), d_normed = lax.scan(grad_rows, zeros_init, (normed.reshape(LAT_TILES, ROWS * LON, D), rounded.reshape(LAT_TILES, ROWS * LON, D)))
    d_scaled = d_normed.reshape(LAT, LON, D) * norm_gain
    mean_grad = lax.optimization_barrier(jnp.mean(d_scaled, axis=-1, keepdims=True))
    mean_cross = lax.optimization_barrier(jnp.mean(d_scaled * scaled, axis=-1, keepdims=True))
    d_taps = (inverse * (d_scaled - mean_grad - scaled * mean_cross)).astype(jnp.bfloat16)

    def conv_of(padded_values, kernel_values):
        return apply_kernel(padded_values, kernel_values, LAT, LON)
    _, conv_pull = jax.vjp(conv_of, padded.astype(jnp.float32), kernel)
    d_padded, kernel_grad = conv_pull(d_taps.astype(jnp.float32))
    _, extend_pull = jax.vjp(lambda values: extend(values, folded), jnp.zeros((LAT, LON, D), jnp.float32))
    spread = extend_pull(d_padded)[0]
    return (spread, kernel_grad / grad_scale, inner_sum / grad_scale, outer_sum / grad_scale)

def tile_blocks(fields):
    depth = fields.shape[-1]
    tiles = fields.reshape(LAT_TILES, ROWS, LON_TILES, COLS, depth).transpose(0, 2, 1, 3, 4)
    return tiles.reshape(LAT_TILES, LON_TILES, NB, 128, depth).transpose(0, 1, 2, 4, 3)

def untile(blocks):
    depth = blocks.shape[3]
    tiles = blocks.transpose(0, 1, 2, 4, 3).reshape(LAT_TILES, LON_TILES, ROWS, COLS, depth)
    return tiles.transpose(0, 2, 1, 3, 4).reshape(LAT, LON, depth)

def remap(blocks, sources, targets, weights):
    sources = sources.astype(jnp.int32)
    targets = targets.astype(jnp.int32)
    offset = sources // (LAT_TILES * NB)
    src_lat = sources // NB % LAT_TILES
    src_block = sources % NB
    src_lon = (jnp.arange(LON_TILES, dtype=jnp.int32)[None, :, None] + offset - 1) % LON_TILES
    picked = blocks[src_lat, src_lon, src_block].astype(jnp.float32)
    placing = (targets[..., None] == jnp.arange(NB, dtype=jnp.int32)).astype(jnp.float32) * weights[..., None]
    return jnp.einsum('nweb,nwekp->nwbkp', placing, picked, precision=highest)

def remap_adjoint(cotangent, sources, targets, weights):
    _, pull = jax.vjp(lambda blocks: remap(blocks, sources, targets, weights), jnp.zeros_like(cotangent))
    return pull(cotangent)[0]

def reference(atmos_state, ocean_state, wet_mask, atmos_kernel, atmos_gain, atmos_inner, atmos_outer, ocean_kernel, ocean_gain, ocean_inner, ocean_outer, flux_head, flux_lift, surface_head, surface_lift, flux_source, flux_target, flux_weight, surface_source, surface_target, surface_weight, atmos_cotangent, ocean_cotangent):
    wet_cells = wet_mask.astype(jnp.float32)[:, :, None]
    surface = jnp.einsum('yxd,dk->yxk', ocean_state.astype(jnp.float32), surface_head.astype(jnp.float32), precision=highest).astype(jnp.bfloat16)
    to_atmos = untile(remap(tile_blocks(surface), surface_source, surface_target, surface_weight))
    atmos_lift = jnp.einsum('yxk,kd->yxd', to_atmos, surface_lift.astype(jnp.float32), precision=highest)
    atmos_start = (atmos_state.astype(jnp.float32) + atmos_lift).astype(jnp.bfloat16)
    atmos_branch, atmos_stored = block_forward(atmos_start, atmos_kernel, atmos_gain, atmos_inner, atmos_outer, False)
    atmos_next = (atmos_start.astype(jnp.float32) + atmos_branch).astype(jnp.bfloat16)
    fluxes = jnp.einsum('yxd,dk->yxk', atmos_next.astype(jnp.float32), flux_head.astype(jnp.float32), precision=highest).astype(jnp.bfloat16)
    to_ocean = untile(remap(tile_blocks(fluxes), flux_source, flux_target, flux_weight))
    ocean_lift = jnp.einsum('yxk,kd->yxd', to_ocean, flux_lift.astype(jnp.float32), precision=highest)
    ocean_start = ((ocean_state.astype(jnp.float32) + ocean_lift) * wet_cells).astype(jnp.bfloat16)
    ocean_branch, ocean_stored = block_forward(ocean_start, ocean_kernel, ocean_gain, ocean_inner, ocean_outer, True)
    ocean_next = ((ocean_start.astype(jnp.float32) + ocean_branch) * wet_cells).astype(jnp.bfloat16)
    ocean_total = ocean_cotangent.astype(jnp.float32) * wet_cells
    ocean_spread, ocean_kernel_grad, ocean_inner_grad, ocean_outer_grad = block_backward(ocean_stored, ocean_kernel, ocean_gain, ocean_inner, ocean_outer, ocean_total, True)
    ocean_start_grad = (ocean_total + ocean_spread) * wet_cells
    flux_target_grad = jnp.einsum('yxd,kd->yxk', ocean_start_grad, flux_lift.astype(jnp.float32), precision=highest)
    flux_grad = untile(remap_adjoint(tile_blocks(flux_target_grad), flux_source, flux_target, flux_weight))
    atmos_total = atmos_cotangent.astype(jnp.float32) + jnp.einsum('yxk,dk->yxd', flux_grad, flux_head.astype(jnp.float32), precision=highest)
    atmos_spread, atmos_kernel_grad, atmos_inner_grad, atmos_outer_grad = block_backward(atmos_stored, atmos_kernel, atmos_gain, atmos_inner, atmos_outer, atmos_total, False)
    atmos_start_grad = atmos_total + atmos_spread
    atmos_state_grad = atmos_start_grad.astype(jnp.bfloat16)
    surface_target_grad = jnp.einsum('yxd,kd->yxk', atmos_start_grad, surface_lift.astype(jnp.float32), precision=highest)
    surface_grad = untile(remap_adjoint(tile_blocks(surface_target_grad), surface_source, surface_target, surface_weight))
    ocean_state_grad = (ocean_start_grad + jnp.einsum('yxk,dk->yxd', surface_grad, surface_head.astype(jnp.float32), precision=highest)).astype(jnp.bfloat16)
    return (atmos_next, ocean_next, atmos_state_grad, ocean_state_grad, atmos_inner_grad, atmos_outer_grad, atmos_kernel_grad, ocean_inner_grad, ocean_outer_grad, ocean_kernel_grad)
```

```python
import jax
import jax.numpy as jnp
from jax import lax
from jax.sharding import PartitionSpec as P

KERNEL = 7


norm_eps = 1e-06
grad_scale = 256.0
highest = lax.Precision.HIGHEST


def pairs_along(axis, bit):
    return [(i, i ^ (1 << bit)) for i in range(lax.axis_size(axis))]


def bits_of(axis):
    return lax.axis_size(axis).bit_length() - 1


def scatter_sum(partial, order):
    labels = [("wide", bit) for bit in reversed(range(bits_of("wide")))]
    labels += [("narrow", bit) for bit in reversed(range(bits_of("narrow")))]
    rows, cols = partial.shape
    running = partial.reshape((2,) * len(labels) + (rows >> len(labels), cols))
    for axis, bit in order:
        dim = labels.index((axis, bit))
        labels.pop(dim)
        mine = (lax.axis_index(axis) >> bit) & 1
        keep = lax.dynamic_index_in_dim(running, mine, dim, keepdims=False)
        away = lax.dynamic_index_in_dim(running, 1 - mine, dim, keepdims=False)
        came = lax.ppermute(away, axis, pairs_along(axis, bit))
        running = keep.astype(jnp.float32) + came.astype(jnp.float32)
        if labels:
            running = running.astype(jnp.bfloat16)
    return running


def full_sum(partial):
    for axis in ("narrow", "wide"):
        for bit in range(bits_of(axis)):
            partial = partial + lax.ppermute(partial, axis, pairs_along(axis, bit))
    return partial


def extended(cells, sides, width, closed):
    for axis, dim in sides:
        count = lax.axis_size(axis)
        ends = count if closed else count - 1
        head = lax.slice_in_dim(cells, 0, width, axis=dim)
        tail = lax.slice_in_dim(cells, cells.shape[dim] - width, cells.shape[dim], axis=dim)
        cells = jnp.concatenate(
            [
                lax.ppermute(tail, axis, [(i, (i + 1) % count) for i in range(ends)]),
                cells,
                lax.ppermute(head, axis, [((i + 1) % count, i) for i in range(ends)]),
            ],
            axis=dim,
        )
    return cells


def normal_cdf(values):
    return 0.5 * (1.0 + lax.erf(values * 0.7071067811865476))


def normal_density(values):
    return jnp.exp(-0.5 * values * values) * 0.3989422804014327


def at_fold():
    return lax.axis_index("narrow") == lax.axis_size("narrow") - 1


def fold_rows(top_band):
    cols, rows = lax.axis_size("wide"), lax.axis_size("narrow")
    pairs = [(w * rows + rows - 1, (cols - 1 - w) * rows + rows - 1) for w in range(cols)]
    return lax.ppermute(top_band, ("wide", "narrow"), pairs)[::-1, ::-1]


def extend(fields, folded):
    margin = KERNEL // 2
    row_count = fields.shape[0]
    beside = extended(fields, (("wide", 1),), margin, True)
    padded = extended(beside, (("narrow", 0),), margin, False)
    if folded:
        mirror = fold_rows(padded[row_count : row_count + margin])
        upper_rows = jnp.where(at_fold(), mirror, padded[row_count + margin :])
        padded = jnp.concatenate([padded[: row_count + margin], upper_rows], axis=0)
    return padded


def apply_kernel(padded, kernel, row_count, col_count, flipped):
    last_tap = KERNEL - 1
    running = jnp.zeros((row_count, col_count, kernel.shape[-1]), jnp.float32)
    for row_tap in range(KERNEL):
        for col_tap in range(KERNEL):
            row_from = last_tap - row_tap if flipped else row_tap
            col_from = last_tap - col_tap if flipped else col_tap
            window = padded[row_from : row_from + row_count, col_from : col_from + col_count]
            running = running + window * kernel[row_tap, col_tap]
    return running


def block_forward(start_field, kernel, norm_gain, inner_weight, outer_weight, folded):
    row_count, col_count, channels = start_field.shape
    padded = extend(start_field, folded)
    mixed_taps = apply_kernel(padded, kernel, row_count, col_count, False)
    center = mixed_taps - jnp.mean(mixed_taps, axis=-1, keepdims=True)
    inverse = lax.rsqrt(jnp.mean(center * center, axis=-1, keepdims=True) + norm_eps)
    scaled = center * inverse
    normed = (scaled * norm_gain).astype(jnp.bfloat16).reshape(-1, channels)
    before = jnp.dot(normed, inner_weight, preferred_element_type=jnp.float32)
    hidden = (before * normal_cdf(before)).astype(jnp.bfloat16)
    branch = jnp.dot(hidden, outer_weight, preferred_element_type=jnp.float32).reshape(
        row_count, col_count, channels
    )
    return (branch, (padded, scaled, inverse, normed, before, hidden))


def block_backward(stored, kernel, norm_gain, inner_weight, outer_weight, incoming, folded):
    padded, scaled, inverse, normed, before, hidden = stored
    row_count, col_count, channels = scaled.shape
    margin = KERNEL // 2
    rounded = incoming.astype(jnp.bfloat16)
    flat_round = rounded.reshape(-1, channels)
    d_hidden = jnp.einsum("cd,fd->cf", flat_round, outer_weight, preferred_element_type=jnp.float32)
    slopes = normal_cdf(before) + before * normal_density(before)
    d_before = (d_hidden * slopes).astype(jnp.bfloat16)
    d_normed = jnp.einsum("cf,df->cd", d_before, inner_weight, preferred_element_type=jnp.float32)
    d_scaled = d_normed.reshape(row_count, col_count, channels) * norm_gain
    mean_grad = jnp.mean(d_scaled, axis=-1, keepdims=True)
    mean_cross = jnp.mean(d_scaled * scaled, axis=-1, keepdims=True)
    d_taps = (inverse * (d_scaled - mean_grad - scaled * mean_cross)).astype(jnp.bfloat16)
    kernel_rows = []
    for row_tap in range(KERNEL):
        for col_tap in range(KERNEL):
            window = padded[row_tap : row_tap + row_count, col_tap : col_tap + col_count]
            kernel_rows.append(
                jnp.einsum("rcd,rcd->d", d_taps, window, preferred_element_type=jnp.float32)
            )
    kernel_term = jnp.stack(kernel_rows).reshape(KERNEL, KERNEL, channels)
    grad_padded = extend(d_taps, folded)
    if folded:
        upper_rows = grad_padded[row_count + margin :]
        blank_rows = jnp.zeros_like(upper_rows)
        top_part = jnp.where(at_fold(), upper_rows, blank_rows)
        lower_rows = jnp.concatenate(
            [grad_padded[: row_count + margin], jnp.where(at_fold(), blank_rows, upper_rows)],
            axis=0,
        )
        spread = apply_kernel(lower_rows, kernel, row_count, col_count, True)
        fold_pad = jnp.concatenate([jnp.zeros_like(grad_padded[: 2 * margin]), top_part], axis=0)
        fold_part = apply_kernel(fold_pad, kernel, margin, col_count, False)
        spread = spread.at[row_count - margin :].add(fold_part)
    else:
        spread = apply_kernel(grad_padded, kernel, row_count, col_count, True)
    return (incoming + spread, (normed, d_before, hidden, flat_round, kernel_term))


def around(tile):
    column = lax.all_gather(tile, "narrow", axis=0, tiled=False)
    return extended(column[None], (("wide", 0),), 1, True)


def remap_matrix(sources, targets, weights, block_count):
    blocks = 3 * lax.axis_size("narrow") * block_count
    placing = (targets[:, None] == jnp.arange(block_count)).astype(jnp.float32) * weights[:, None]
    choose = (sources[:, None] == jnp.arange(blocks)).astype(jnp.float32)
    return jnp.einsum("eb,es->bs", placing, choose, precision=highest)


def adjoint_matrix(lists, block_count):
    sources, targets, weights = lists
    lat_count = lax.axis_size("narrow")
    own = lax.axis_index("narrow")
    offset = 2 - jnp.arange(3)
    first = (offset[:, None, None] * lat_count + own) * block_count
    local = (sources - first)[..., None]
    choose = (local == jnp.arange(block_count)).astype(jnp.float32) * weights[..., None]
    placing = (targets[..., None] == jnp.arange(block_count)).astype(jnp.float32)
    return jnp.einsum("ones,oneb->sonb", choose, placing, precision=highest).reshape(block_count, -1)


def remap(matrix, fields):
    flat_blocks = around(fields).reshape(-1, fields.shape[1], fields.shape[2])
    return jnp.einsum("bs,skp->bkp", matrix, flat_blocks.astype(jnp.float32), precision=highest)


def to_cells(blocks, lift_weight, row_count, col_count):
    lifted = jnp.einsum("bkp,kd->bpd", blocks, lift_weight.astype(jnp.float32), precision=highest)
    return lifted.reshape(row_count, col_count, lift_weight.shape[1])


def lift_back(gradient, lift_weight):
    return jnp.einsum(
        "bpd,kd->bkp",
        gradient.reshape(-1, 128, lift_weight.shape[1]),
        lift_weight.astype(jnp.float32),
        precision=highest,
    )


def head_back(gradient, head_weight, row_count, col_count):
    spread = jnp.einsum("bkp,dk->bpd", gradient, head_weight.astype(jnp.float32), precision=highest)
    return spread.reshape(row_count, col_count, head_weight.shape[0])


def weight_sums(record):
    normed, d_before, hidden, flat_round, _ = record
    inner_part = lax.dot_general(
        normed, d_before, (((0,), (0,)), ((), ())), preferred_element_type=jnp.float32
    ).astype(jnp.bfloat16)
    outer_part = lax.dot_general(
        hidden, flat_round, (((0,), (0,)), ((), ())), preferred_element_type=jnp.float32
    ).astype(jnp.bfloat16)
    wide_bits = [("wide", bit) for bit in range(bits_of("wide"))]
    narrow_bits = [("narrow", bit) for bit in range(bits_of("narrow"))]
    one = narrow_bits + wide_bits
    other = narrow_bits[:1] + wide_bits[:1] + narrow_bits[1:] + wide_bits[1:]
    return scatter_sum(inner_part, one) / grad_scale, scatter_sum(outer_part, other) / grad_scale


def per_device(
    atmos_state,
    ocean_state,
    wet_mask,
    atmos_kernel,
    atmos_gain,
    atmos_inner,
    atmos_outer,
    ocean_kernel,
    ocean_gain,
    ocean_inner,
    ocean_outer,
    flux_head,
    flux_lift,
    surface_head,
    surface_lift,
    flux_source,
    flux_target,
    flux_weight,
    surface_source,
    surface_target,
    surface_weight,
    atmos_cotangent,
    ocean_cotangent,
):
    row_count, col_count, channels = atmos_state.shape
    wet_cells = wet_mask.astype(jnp.float32)[:, :, None]
    block_count = row_count * col_count // 128
    flux_lists = (flux_source.reshape(-1), flux_target.reshape(-1), flux_weight.reshape(-1))
    surface_lists = (
        surface_source.reshape(-1),
        surface_target.reshape(-1),
        surface_weight.reshape(-1),
    )
    flux_matrix = remap_matrix(*flux_lists, block_count)
    surface_matrix = remap_matrix(*surface_lists, block_count)
    lists = jnp.stack([part.astype(jnp.float32) for part in flux_lists + surface_lists])
    lists = jnp.moveaxis(around(lists), 2, 0)
    flux_adjoint = adjoint_matrix(lists[:3], block_count)
    surface_adjoint = adjoint_matrix(lists[3:], block_count)
    surface = jnp.einsum(
        "bpd,dk->bkp",
        ocean_state.reshape(-1, 128, channels),
        surface_head,
        preferred_element_type=jnp.float32,
    ).astype(jnp.bfloat16)
    to_atmos = remap(surface_matrix, surface)
    atmos_start = (atmos_state + to_cells(to_atmos, surface_lift, row_count, col_count)).astype(
        jnp.bfloat16
    )
    atmos_branch, atmos_stored = block_forward(
        atmos_start, atmos_kernel, atmos_gain, atmos_inner, atmos_outer, False
    )
    atmos_next = (atmos_start + atmos_branch).astype(jnp.bfloat16)
    fluxes = jnp.einsum(
        "bpd,dk->bkp",
        atmos_next.reshape(-1, 128, channels),
        flux_head,
        preferred_element_type=jnp.float32,
    ).astype(jnp.bfloat16)
    to_ocean = remap(flux_matrix, fluxes)
    ocean_start = (
        (ocean_state + to_cells(to_ocean, flux_lift, row_count, col_count)) * wet_cells
    ).astype(jnp.bfloat16)
    ocean_branch, ocean_stored = block_forward(
        ocean_start, ocean_kernel, ocean_gain, ocean_inner, ocean_outer, True
    )
    ocean_next = ((ocean_start + ocean_branch) * wet_cells).astype(jnp.bfloat16)
    ocean_total = ocean_cotangent * wet_cells
    ocean_start_grad, ocean_record = block_backward(
        ocean_stored, ocean_kernel, ocean_gain, ocean_inner, ocean_outer, ocean_total, True
    )
    ocean_start_grad = ocean_start_grad * wet_cells
    flux_grad = remap(flux_adjoint, lift_back(ocean_start_grad, flux_lift).astype(jnp.bfloat16))
    atmos_total = atmos_cotangent + head_back(flux_grad, flux_head, row_count, col_count)
    atmos_start_grad, atmos_record = block_backward(
        atmos_stored, atmos_kernel, atmos_gain, atmos_inner, atmos_outer, atmos_total, False
    )
    atmos_state_grad = atmos_start_grad.astype(jnp.bfloat16)
    surface_grad = remap(surface_adjoint, lift_back(atmos_start_grad, surface_lift).astype(jnp.bfloat16))
    ocean_state_grad = (
        ocean_start_grad + head_back(surface_grad, surface_head, row_count, col_count)
    ).astype(jnp.bfloat16)
    ocean_sums = weight_sums(ocean_record)
    atmos_sums = weight_sums(atmos_record)
    kernel_sums = full_sum(jnp.stack([atmos_record[4], ocean_record[4]])) / grad_scale
    return (
        atmos_next,
        ocean_next,
        atmos_state_grad,
        ocean_state_grad,
        atmos_sums[0],
        atmos_sums[1],
        kernel_sums[0],
        ocean_sums[0],
        ocean_sums[1],
        kernel_sums[1],
    )


def solution(mesh):
    return jax.shard_map(
        per_device,
        mesh=mesh,
        in_specs=(
            P("narrow", "wide", None),
            P("narrow", "wide", None),
            P("narrow", "wide"),
            P(),
            P(),
            P(),
            P(),
            P(),
            P(),
            P(),
            P(),
            P(),
            P(),
            P(),
            P(),
            P("narrow", "wide", None),
            P("narrow", "wide", None),
            P("narrow", "wide", None),
            P("narrow", "wide", None),
            P("narrow", "wide", None),
            P("narrow", "wide", None),
            P("narrow", "wide", None),
            P("narrow", "wide", None),
        ),
        out_specs=(
            P("narrow", "wide", None),
            P("narrow", "wide", None),
            P("narrow", "wide", None),
            P("narrow", "wide", None),
            P(("wide", "narrow"), None),
            P(("wide", "narrow"), None),
            P(),
            P(("wide", "narrow"), None),
            P(("wide", "narrow"), None),
            P(),
        ),
        check_vma=False,
    )
```

```python
import functools

import jax
import jax.numpy as jnp
from jax import lax
from jax.experimental import pallas as pl
from jax.experimental.pallas import tpu as pltpu
from jax.sharding import PartitionSpec as P

KERNEL = 7
TAPS = KERNEL * KERNEL
MARGIN = KERNEL // 2
LANES = 128
SIDE = 16

norm_eps = 1e-06
grad_scale = 256.0
highest = lax.Precision.HIGHEST


def pairs_along(axis, bit):
    return [(i, i ^ (1 << bit)) for i in range(lax.axis_size(axis))]


def bits_of(axis):
    return lax.axis_size(axis).bit_length() - 1


def scatter_sum(partial, order):
    labels = [("wide", bit) for bit in reversed(range(bits_of("wide")))]
    labels += [("narrow", bit) for bit in reversed(range(bits_of("narrow")))]
    rows, cols = partial.shape
    running = partial.reshape((2,) * len(labels) + (rows >> len(labels), cols))
    for axis, bit in order:
        dim = labels.index((axis, bit))
        labels.pop(dim)
        mine = (lax.axis_index(axis) >> bit) & 1
        keep = lax.dynamic_index_in_dim(running, mine, dim, keepdims=False)
        away = lax.dynamic_index_in_dim(running, 1 - mine, dim, keepdims=False)
        came = lax.ppermute(away, axis, pairs_along(axis, bit))
        running = keep.astype(jnp.float32) + came.astype(jnp.float32)
        if labels:
            running = running.astype(jnp.bfloat16)
    return running


def full_sum(partial):
    for axis in ("narrow", "wide"):
        for bit in range(bits_of(axis)):
            partial = partial + lax.ppermute(partial, axis, pairs_along(axis, bit))
    return partial


def shift_pairs(axis, step, closed):
    count = lax.axis_size(axis)
    return [(i, (i + step) % count) for i in range(count) if closed or 0 <= i + step < count]


def from_sides(cells, axis, dim, width, closed):
    head = lax.slice_in_dim(cells, 0, width, axis=dim)
    tail = lax.slice_in_dim(cells, cells.shape[dim] - width, cells.shape[dim], axis=dim)
    return (
        lax.ppermute(tail, axis, shift_pairs(axis, 1, closed)),
        lax.ppermute(head, axis, shift_pairs(axis, -1, closed)),
    )


def normal_cdf(values):
    return 0.5 * (1.0 + lax.erf(values * 0.7071067811865476))


def normal_density(values):
    return jnp.exp(-0.5 * values * values) * 0.3989422804014327


def fold_band(beside):
    cols, rows = lax.axis_size("wide"), lax.axis_size("narrow")
    pairs = [(w * rows + rows - 1, (cols - 1 - w) * rows + rows - 1) for w in range(cols)]
    band = beside[beside.shape[0] - MARGIN :][::-1]
    length = band.shape[1]
    turn = jnp.arange(length)[:, None] + jnp.arange(length)[None, :] == length - 1
    turned = jnp.einsum(
        "ij,rjd->rid", turn.astype(band.dtype), band, preferred_element_type=jnp.float32
    ).astype(band.dtype)
    return lax.ppermute(turned, ("wide", "narrow"), pairs)


def roomy(padded):
    return jnp.pad(padded, ((0, 0), (0, SIDE - 2 * MARGIN), (0, 0)))


def extend(fields, folded):
    left, right = from_sides(fields, "wide", 1, MARGIN, True)
    beside = jnp.concatenate([left, fields, right], axis=1)
    below, above = from_sides(beside, "narrow", 0, MARGIN, False)
    mirror = fold_band(beside) if folded else None
    return jnp.concatenate([below, beside, above], axis=0), mirror


def spread_taps(kernel_ref, spread_ref, flipped):
    for tap in range(TAPS):
        place = TAPS - 1 - tap if flipped else tap
        row = kernel_ref[tap // KERNEL, pl.ds(tap % KERNEL, 1), :]
        spread_ref[place] = jnp.broadcast_to(row, spread_ref.shape[1:])


def convolve(wide_ref, first, spread_ref, out_ref):
    row_count, col_count, _ = out_ref.shape
    groups = (col_count // 8, 8, LANES)

    def one_row(row, sums, least, most):
        sums = list(sums)
        for b in range(KERNEL):
            cells = wide_ref[first + row, b : b + col_count, :].reshape(groups)
            for a in range(least, most):
                sums[a] = sums[a] + cells * spread_ref[a * KERNEL + b]
        return sums

    def finish(row, sums):
        out_ref[row - KERNEL + 1] = sums[-1].reshape(col_count, LANES)
        return [jnp.zeros(groups, jnp.float32), *sums[:-1]]

    sums = [jnp.zeros(groups, jnp.float32)] * KERNEL
    for row in range(KERNEL - 1):
        sums = one_row(row, sums, 0, row + 1)
        sums = [jnp.zeros(groups, jnp.float32), *sums[:-1]]

    def two_rows(pair, sums):
        for half in range(2):
            row = KERNEL - 1 + 2 * pair + half
            sums = finish(row, one_row(row, sums, 0, KERNEL))
        return tuple(sums)

    pairs = (row_count - KERNEL + 1) // 2
    sums = lax.fori_loop(0, pairs, two_rows, tuple(sums))
    for row in range(KERNEL - 1 + 2 * pairs, row_count + KERNEL - 1):
        sums = finish(row, one_row(row, sums, max(0, row - row_count + 1), KERNEL))


def conv_body(flipped, padded_ref, kernel_ref, out_ref, wide_ref, spread_ref):
    wide_ref[...] = padded_ref[...].astype(jnp.float32)
    spread_taps(kernel_ref, spread_ref, flipped)
    convolve(wide_ref, 0, spread_ref, out_ref)


def apply_kernel(padded, kernel, row_count, col_count, flipped):
    rows, cols, channels = padded.shape
    return pl.pallas_call(
        functools.partial(conv_body, flipped),
        grid=(channels // LANES,),
        in_specs=[
            pl.BlockSpec((rows, cols, LANES), lambda g: (0, 0, g)),
            pl.BlockSpec((KERNEL, KERNEL, LANES), lambda g: (0, 0, g)),
        ],
        out_specs=pl.BlockSpec((row_count, col_count, LANES), lambda g: (0, 0, g)),
        out_shape=jax.ShapeDtypeStruct((row_count, col_count, channels), jnp.float32),
        scratch_shapes=[
            pltpu.VMEM((rows, cols, LANES), jnp.float32),
            pltpu.VMEM((TAPS, 8, LANES), jnp.float32),
        ],
        cost_estimate=pl.CostEstimate(flops=9 * 10**9, bytes_accessed=3 << 20, transcendentals=0),
        compiler_params=pltpu.CompilerParams(vmem_limit_bytes=32 << 20),
        name="depthwise",
    )(padded, kernel)


def fold_body(band_ref, kernel_ref, out_ref, wide_ref):
    _, col_count, _ = out_ref.shape
    wide_ref[...] = band_ref[...].astype(jnp.float32)
    for row in range(MARGIN):
        total = jnp.zeros((col_count, LANES), jnp.float32)
        for band in range(row + 1):
            for b in range(KERNEL):
                tap = kernel_ref[KERNEL - 1 + band - row, pl.ds(b, 1), :]
                total = total + wide_ref[band, b : b + col_count, :] * tap
        out_ref[row] = total


def fold_taps(band, kernel, col_count):
    rows, cols, channels = band.shape
    return pl.pallas_call(
        fold_body,
        grid=(channels // LANES,),
        in_specs=[
            pl.BlockSpec((rows, cols, LANES), lambda g: (0, 0, g)),
            pl.BlockSpec((KERNEL, KERNEL, LANES), lambda g: (0, 0, g)),
        ],
        out_specs=pl.BlockSpec((rows, col_count, LANES), lambda g: (0, 0, g)),
        out_shape=jax.ShapeDtypeStruct((rows, col_count, channels), jnp.float32),
        scratch_shapes=[pltpu.VMEM((rows, cols, LANES), jnp.float32)],
        compiler_params=pltpu.CompilerParams(vmem_limit_bytes=16 << 20),
        name="fold_taps",
    )(band, kernel)


def kernel_grad_body(grad_ref, padded_ref, out_ref, wide_ref, tall_ref, sums_ref):
    row_count, col_count, _ = grad_ref.shape
    border = KERNEL - 1
    groups = (col_count // 8, 8, LANES)
    wide_ref[...] = padded_ref[...].astype(jnp.float32)
    tall_ref[:border] = jnp.zeros((border, col_count, LANES), jnp.float32)
    tall_ref[border : border + row_count] = grad_ref[...].astype(jnp.float32)
    tall_ref[border + row_count :] = jnp.zeros((border, col_count, LANES), jnp.float32)
    sums_ref[...] = jnp.zeros_like(sums_ref)

    def one_row(row, carry):
        grads = [tall_ref[row + border - a].reshape(groups) for a in range(KERNEL)]
        for b in range(KERNEL):
            cells = wide_ref[row, b : b + col_count, :].reshape(groups)
            for a in range(KERNEL):
                sums_ref[a * KERNEL + b] += jnp.sum(grads[a] * cells, axis=0)
        return carry

    lax.fori_loop(0, row_count + border, one_row, 0)
    out_ref[...] = jnp.sum(sums_ref[...], axis=1)


def kernel_grad(grads, padded):
    rows, cols, channels = padded.shape
    row_count, col_count, _ = grads.shape
    return pl.pallas_call(
        kernel_grad_body,
        grid=(channels // LANES,),
        in_specs=[
            pl.BlockSpec((row_count, col_count, LANES), lambda g: (0, 0, g)),
            pl.BlockSpec((rows, cols, LANES), lambda g: (0, 0, g)),
        ],
        out_specs=pl.BlockSpec((TAPS, LANES), lambda g: (0, g)),
        out_shape=jax.ShapeDtypeStruct((TAPS, channels), jnp.float32),
        scratch_shapes=[
            pltpu.VMEM((rows, cols, LANES), jnp.float32),
            pltpu.VMEM((row_count + 2 * (KERNEL - 1), col_count, LANES), jnp.float32),
            pltpu.VMEM((TAPS, 8, LANES), jnp.float32),
        ],
        cost_estimate=pl.CostEstimate(flops=9 * 10**9, bytes_accessed=3 << 20, transcendentals=0),
        compiler_params=pltpu.CompilerParams(vmem_limit_bytes=32 << 20),
        name="kernel_grad",
    )(grads, padded)


def block_forward(
    padded, mixed_taps, mirror, start_field, kernel, norm_gain, inner_weight, outer_weight
):
    row_count, col_count, channels = start_field.shape
    if mirror is not None:
        mixed_taps = mixed_taps.at[row_count - MARGIN :].add(fold_taps(mirror, kernel, col_count))
        padded = padded.at[row_count + MARGIN :].add(mirror)
    center = mixed_taps - jnp.mean(mixed_taps, axis=-1, keepdims=True)
    inverse = lax.rsqrt(jnp.mean(center * center, axis=-1, keepdims=True) + norm_eps)
    scaled = center * inverse
    normed = (scaled * norm_gain).astype(jnp.bfloat16).reshape(-1, channels)
    before = jnp.dot(normed, inner_weight, preferred_element_type=jnp.float32)
    hidden = (before * normal_cdf(before)).astype(jnp.bfloat16)
    branch = jnp.dot(hidden, outer_weight, preferred_element_type=jnp.float32).reshape(
        row_count, col_count, channels
    )
    return (branch, (padded, scaled, inverse, normed, before, hidden))


def block_backward(stored, kernel, norm_gain, inner_weight, outer_weight, incoming, folded):
    padded, scaled, inverse, normed, before, hidden = stored
    row_count, col_count, channels = scaled.shape
    rounded = incoming.astype(jnp.bfloat16)
    flat_round = rounded.reshape(-1, channels)
    d_hidden = jnp.einsum("cd,fd->cf", flat_round, outer_weight, preferred_element_type=jnp.float32)
    slopes = normal_cdf(before) + before * normal_density(before)
    d_before = (d_hidden * slopes).astype(jnp.bfloat16)
    d_normed = jnp.einsum("cf,df->cd", d_before, inner_weight, preferred_element_type=jnp.float32)
    d_scaled = d_normed.reshape(row_count, col_count, channels) * norm_gain
    mean_grad = jnp.mean(d_scaled, axis=-1, keepdims=True)
    mean_cross = jnp.mean(d_scaled * scaled, axis=-1, keepdims=True)
    d_taps = (inverse * (d_scaled - mean_grad - scaled * mean_cross)).astype(jnp.bfloat16)
    kernel_term = kernel_grad(d_taps, padded).reshape(KERNEL, KERNEL, channels)
    grad_padded, mirror = extend(d_taps, folded)
    spread = apply_kernel(roomy(grad_padded), kernel, row_count, col_count, True)
    if folded:
        fold_part = fold_taps(roomy(mirror), kernel, col_count)
        spread = spread.at[row_count - MARGIN :].add(fold_part)
    return (incoming + spread, (normed, d_before, hidden, flat_round, kernel_term))


def around(tile, reach):
    column = lax.all_gather(tile, "narrow", axis=0, tiled=False)
    return [
        lax.ppermute(column, "wide", shift_pairs("wide", -offset, True)) if offset else column
        for offset in range(-reach, reach + 1)
    ]


def across(lhs, rhs):
    return lax.dot_general(lhs, rhs, (((1,), (1,)), ((), ())), preferred_element_type=jnp.float32)


def three_parts(values):
    parts = []
    for _ in range(3):
        part = values.astype(jnp.bfloat16)
        parts.append(part)
        values = values - part.astype(jnp.float32)
    return jnp.concatenate([part.astype(jnp.float32) for part in parts]).astype(jnp.bfloat16)


def summed(stacked):
    count = stacked.shape[0] // 3
    return stacked[:count] + stacked[count : 2 * count] + stacked[2 * count :]


def head_body(with_lists, state_ref, head_ref, *refs):
    out_ref = refs[-1]
    blocks = state_ref.shape[0] // LANES
    fields = head_ref.shape[0]
    rows = [
        across(head_ref[...], state_ref[pl.ds(block * LANES, LANES), :]) for block in range(blocks)
    ]
    if with_lists:
        lists = refs[0][...]
        for first in (0, 3):
            rows.append(lists[first : first + 2])
            rows.append(three_parts(lists[first + 2 : first + 3]).astype(jnp.float32))
        rows.append(jnp.zeros((out_ref.shape[0] - blocks * fields - 10, LANES), jnp.float32))
    out_ref[...] = jnp.concatenate(rows).astype(jnp.bfloat16)


def coupled_fields(state, head_rows, lists=None):
    cells, channels = state.shape
    rows = cells // LANES * head_rows.shape[0] + (0 if lists is None else 16)
    operands = [state, head_rows] + ([] if lists is None else [lists])
    return pl.pallas_call(
        functools.partial(head_body, lists is not None),
        out_shape=jax.ShapeDtypeStruct((rows, LANES), jnp.bfloat16),
        compiler_params=pltpu.CompilerParams(vmem_limit_bytes=16 << 20),
        name="coupled_fields",
    )(*operands)


def list_of(lists_ref, tile, which, first):
    rows = lists_ref[tile, first:, :].astype(jnp.float32)[5 * which : 5 * which + 5]
    return rows[0:1].astype(jnp.int32), rows[1:2].astype(jnp.int32), [rows[i : i + 1] for i in (2, 3, 4)]


def rows_like(index, parts, count):
    at = lax.broadcasted_iota(jnp.int32, (count, LANES), 0) == index
    return jnp.concatenate([jnp.where(at, part, 0.0) for part in parts]).astype(jnp.bfloat16)


def chosen(index):
    at = lax.broadcasted_iota(jnp.int32, (LANES, LANES), 0) == index
    return jnp.where(at, 1.0, 0.0).astype(jnp.bfloat16)


def remap_blocks(matrix, blocks_refs, cells_ref, sums_ref, fields, used):
    cells_ref[...] = jnp.zeros_like(cells_ref)
    lat_count = blocks_refs[0].shape[0]
    for i, ref in enumerate(blocks_refs):
        for tile in range(lat_count):
            cells_ref[pl.ds((i * lat_count + tile) * used, used), :] = ref[tile, :used, :].astype(jnp.float32)
    parts = three_parts(matrix)
    for k in range(fields):
        blocks = cells_ref[pl.ds(k, LANES, stride=fields), :].astype(jnp.bfloat16)
        mixed = jnp.dot(parts, blocks, preferred_element_type=jnp.float32)
        sums_ref[pl.ds(k, matrix.shape[0], stride=fields), :] = summed(mixed)


def lift_block(sums, weights):
    parts = three_parts(sums)
    return lax.dot_general(
        parts,
        jnp.concatenate([weights.astype(jnp.float32)] * 3).astype(jnp.bfloat16),
        (((0,), (0,)), ((), ())),
        preferred_element_type=jnp.float32,
    )


def start_body(which, masked, own_ref, *refs):
    lists, blocks = refs[:3], refs[3:8]
    state_ref, lift_ref, kernel_ref = refs[8:11]
    padded_ref, start_ref, taps_ref = refs[11:14]
    cells_ref, sums_ref, block_ref, wide_ref, spread_ref, wet_ref = refs[14:]
    lat_count = blocks[0].shape[0]
    row_count, col_count, _ = taps_ref.shape
    fields = lift_ref.shape[0]
    block_rows = LANES // col_count
    count = row_count // block_rows
    used = count * fields
    extra = block_rows - MARGIN
    own = own_ref[0]

    @pl.when(pl.program_id(0) == 0)
    def _():
        matrix = []
        for column in range(3):
            mixed = jnp.zeros((3 * (count + 2), LANES), jnp.float32)
            for beside in (-1, 0, 1):
                tile = own + beside
                inside = jnp.where((tile >= 0) & (tile < lat_count), 1.0, 0.0)
                sources, targets, parts = list_of(
                    lists[column], jnp.clip(tile, 0, lat_count - 1), which, used
                )
                placing = rows_like(
                    targets + 1 + beside * count, [part * inside for part in parts], count + 2
                )
                mixed = mixed + across(placing, chosen(sources + column * lat_count * count))
            matrix.append(summed(mixed))
        remap_blocks(jnp.concatenate(matrix), blocks, cells_ref, sums_ref, fields, used)
        if masked:
            wet = jnp.where(state_ref[:, :, 0:1].astype(jnp.float32) < 100.0, 1.0, 0.0)
            wet_ref[...] = jnp.broadcast_to(wet, wet_ref.shape)

    wide_ref[...] = jnp.zeros_like(wide_ref)
    left, right = col_count + MARGIN, col_count + 2 * MARGIN
    for column in range(3):
        for block in range(count + 2):
            sums = sums_ref[pl.ds((column * (count + 2) + block) * fields, fields), :]
            block_ref[...] = lift_block(sums, lift_ref[...]).reshape(block_ref.shape)
            rows = slice(block * block_rows, (block + 1) * block_rows)
            if column == 0:
                wide_ref[rows, 0:MARGIN, :] = block_ref[:, col_count - MARGIN : col_count, :]
            elif column == 1:
                wide_ref[rows, MARGIN : MARGIN + col_count, :] = block_ref[...]
            else:
                wide_ref[rows, left:right, :] = block_ref[:, 0:MARGIN, :]
    rows = slice(extra, extra + row_count + 2 * MARGIN)
    start = state_ref[...].astype(jnp.float32) + wide_ref[rows]
    if masked:
        start = jnp.where(wet_ref[...] > 0.5, start, 0.0)
    start = start.astype(jnp.bfloat16)
    padded_ref[...] = start
    wide_ref[rows] = start.astype(jnp.float32)
    inner = slice(extra + MARGIN, extra + MARGIN + row_count)
    start_ref[...] = wide_ref[inner, MARGIN : MARGIN + col_count, :].astype(jnp.bfloat16)
    spread_taps(kernel_ref, spread_ref, False)
    convolve(wide_ref, extra, spread_ref, taps_ref)


def start_and_taps(which, masked, own, lists, blocks, state, lift_weight, kernel, row_count, col_count):
    rows, cols, channels = state.shape
    fields = lift_weight.shape[0]
    block_rows = LANES // col_count
    count = row_count // block_rows + 2
    whole = lambda part: pl.BlockSpec(part.shape, lambda g: (0, 0, 0))
    return pl.pallas_call(
        functools.partial(start_body, which, masked),
        grid=(channels // LANES,),
        in_specs=[
            pl.BlockSpec(memory_space=pltpu.SMEM),
            *[whole(part) for part in lists],
            *[whole(part) for part in blocks],
            pl.BlockSpec((rows, cols, LANES), lambda g: (0, 0, g)),
            pl.BlockSpec((fields, LANES), lambda g: (0, g)),
            pl.BlockSpec((KERNEL, KERNEL, LANES), lambda g: (0, 0, g)),
        ],
        out_specs=[
            pl.BlockSpec((rows, cols, LANES), lambda g: (0, 0, g)),
            pl.BlockSpec((row_count, col_count, LANES), lambda g: (0, 0, g)),
            pl.BlockSpec((row_count, col_count, LANES), lambda g: (0, 0, g)),
        ],
        out_shape=[
            jax.ShapeDtypeStruct((rows, cols, channels), jnp.bfloat16),
            jax.ShapeDtypeStruct((row_count, col_count, channels), jnp.bfloat16),
            jax.ShapeDtypeStruct((row_count, col_count, channels), jnp.float32),
        ],
        scratch_shapes=[
            pltpu.VMEM((LANES * fields, LANES), jnp.float32),
            pltpu.VMEM((3 * count * fields, LANES), jnp.float32),
            pltpu.VMEM((block_rows, col_count, LANES), jnp.float32),
            pltpu.VMEM((count * block_rows, cols, LANES), jnp.float32),
            pltpu.VMEM((TAPS, 8, LANES), jnp.float32),
            pltpu.VMEM((rows, cols, LANES), jnp.float32),
        ],
        cost_estimate=pl.CostEstimate(flops=10**10, bytes_accessed=3 << 20, transcendentals=0),
        compiler_params=pltpu.CompilerParams(vmem_limit_bytes=32 << 20),
        name="start_and_taps",
    )(own, *lists, *blocks, state, lift_weight, kernel)


def total_body(which, first, own_ref, *refs):
    lists, blocks = refs[:3], refs[3:6]
    head_ref, base_ref, out_ref, cells_ref, sums_ref = refs[6:]
    lat_count = blocks[0].shape[0]
    fields = head_ref.shape[0]
    count = base_ref.shape[0] // LANES
    own = own_ref[0]
    mixed = jnp.zeros((24, LANES), jnp.float32)
    for column in range(3):
        for tile in range(lat_count):
            sources, targets, parts = list_of(lists[column], tile, which, first)
            local = sources - ((2 - column) * lat_count + own) * count
            local = jnp.where(local < count, local, -1)
            place = chosen(targets + (column * lat_count + tile) * count)
            mixed = mixed + across(rows_like(local, parts, 8), place)
    remap_blocks(summed(mixed), blocks, cells_ref, sums_ref, fields, count * fields)
    for block in range(count):
        rows = pl.ds(block * LANES, LANES)
        back = lift_block(sums_ref[pl.ds(block * fields, fields), :], head_ref[...])
        out_ref[rows, :] = (base_ref[rows, :].astype(jnp.float32) + back).astype(out_ref.dtype)


def add_remap_adjoint(which, own, lists, blocks, head_rows, base, kind):
    fields = head_rows.shape[0]
    first = base.shape[0] // LANES * fields
    memory = pl.BlockSpec(memory_space=pltpu.VMEM)
    return pl.pallas_call(
        functools.partial(total_body, which, first),
        in_specs=[pl.BlockSpec(memory_space=pltpu.SMEM)] + [memory] * 8,
        out_shape=jax.ShapeDtypeStruct(base.shape, kind),
        scratch_shapes=[
            pltpu.VMEM((LANES * fields, LANES), jnp.float32),
            pltpu.VMEM((8 * fields, LANES), jnp.float32),
        ],
        compiler_params=pltpu.CompilerParams(vmem_limit_bytes=32 << 20),
        name="add_remap_adjoint",
    )(own, *lists, *blocks, head_rows, base)


def extended_states(states):
    beside = [(lax.ppermute(part, "wide", shift_pairs("wide", step, True))) for part, step in (
        (states[:, :, states.shape[2] - MARGIN :], 1), (states[:, :, :MARGIN], -1))]
    states = jnp.concatenate([beside[0], states, beside[1]], axis=2)
    ends = [(lax.ppermute(part, "narrow", shift_pairs("narrow", step, False))) for part, step in (
        (states[:, states.shape[1] - MARGIN :], 1), (states[:, :MARGIN], -1))]
    states = jnp.concatenate([ends[0], states, ends[1]], axis=1)
    return jnp.pad(states, ((0, 0), (0, 0), (0, SIDE - 2 * MARGIN), (0, 0)))


def lift_back(gradient, lift_weight):
    return jnp.einsum(
        "bpd,kd->bkp",
        gradient.reshape(-1, 128, lift_weight.shape[1]),
        lift_weight.astype(jnp.float32),
        precision=highest,
    )


def weight_sums(record):
    normed, d_before, hidden, flat_round, _ = record
    inner_part = lax.dot_general(
        normed, d_before, (((0,), (0,)), ((), ())), preferred_element_type=jnp.float32
    ).astype(jnp.bfloat16)
    outer_part = lax.dot_general(
        hidden, flat_round, (((0,), (0,)), ((), ())), preferred_element_type=jnp.float32
    ).astype(jnp.bfloat16)
    wide_bits = [("wide", bit) for bit in range(bits_of("wide"))]
    narrow_bits = [("narrow", bit) for bit in range(bits_of("narrow"))]
    one = narrow_bits + wide_bits
    other = narrow_bits[:1] + wide_bits[:1] + narrow_bits[1:] + wide_bits[1:]
    return scatter_sum(inner_part, one) / grad_scale, scatter_sum(outer_part, other) / grad_scale


def per_device(
    atmos_state,
    ocean_state,
    wet_mask,
    atmos_kernel,
    atmos_gain,
    atmos_inner,
    atmos_outer,
    ocean_kernel,
    ocean_gain,
    ocean_inner,
    ocean_outer,
    flux_head,
    flux_lift,
    surface_head,
    surface_lift,
    flux_source,
    flux_target,
    flux_weight,
    surface_source,
    surface_target,
    surface_weight,
    atmos_cotangent,
    ocean_cotangent,
):
    row_count, col_count, channels = atmos_state.shape
    wet_cells = wet_mask.astype(jnp.float32)[:, :, None]
    own = lax.axis_index("narrow").reshape(1).astype(jnp.int32)
    lists = [flux_source, flux_target, flux_weight, surface_source, surface_target, surface_weight]
    lists = jnp.concatenate([part.reshape(1, -1).astype(jnp.float32) for part in lists])
    lists = jnp.pad(lists, ((0, 2), (0, LANES - lists.shape[1])))
    flux_rows, surface_rows = flux_head.T, surface_head.T
    cells = row_count * col_count
    first = around(coupled_fields(ocean_state.reshape(cells, channels), surface_rows, lists), 2)
    lists = first[1:4]
    marked = jnp.where(wet_mask[:, :, None] > 0, ocean_state, jnp.bfloat16(1024.0))
    atmos_wide, ocean_wide = extended_states(jnp.stack([atmos_state, marked]))
    atmos_padded, atmos_start, atmos_taps = start_and_taps(
        1, False, own, lists, first, atmos_wide, surface_lift, atmos_kernel, row_count, col_count
    )
    atmos_branch, atmos_stored = block_forward(
        atmos_padded, atmos_taps, None, atmos_start, atmos_kernel, atmos_gain, atmos_inner, atmos_outer
    )
    atmos_next = (atmos_start + atmos_branch).astype(jnp.bfloat16)
    fluxes = around(coupled_fields(atmos_next.reshape(cells, channels), flux_rows), 2)
    ocean_padded, ocean_start, ocean_taps = start_and_taps(
        0, True, own, lists, fluxes, ocean_wide, flux_lift, ocean_kernel, row_count, col_count
    )
    own_rows = slice(MARGIN, MARGIN + row_count)
    mirror = roomy(fold_band(ocean_padded[own_rows, : col_count + 2 * MARGIN]))
    ocean_branch, ocean_stored = block_forward(
        ocean_padded, ocean_taps, mirror, ocean_start, ocean_kernel, ocean_gain, ocean_inner, ocean_outer
    )
    ocean_next = ((ocean_start + ocean_branch) * wet_cells).astype(jnp.bfloat16)
    ocean_total = ocean_cotangent * wet_cells
    ocean_start_grad, ocean_record = block_backward(
        ocean_stored, ocean_kernel, ocean_gain, ocean_inner, ocean_outer, ocean_total, True
    )
    ocean_start_grad = ocean_start_grad * wet_cells
    flux_grads = lift_back(ocean_start_grad, flux_lift).astype(jnp.bfloat16)
    flux_grads = around(flux_grads.reshape(-1, LANES), 1)
    atmos_total = add_remap_adjoint(
        0, own, lists, flux_grads, flux_rows, atmos_cotangent.reshape(cells, channels), jnp.float32
    ).reshape(row_count, col_count, channels)
    atmos_start_grad, atmos_record = block_backward(
        atmos_stored, atmos_kernel, atmos_gain, atmos_inner, atmos_outer, atmos_total, False
    )
    atmos_state_grad = atmos_start_grad.astype(jnp.bfloat16)
    surface_grads = lift_back(atmos_start_grad, surface_lift).astype(jnp.bfloat16)
    surface_grads = around(surface_grads.reshape(-1, LANES), 1)
    ocean_state_grad = add_remap_adjoint(
        1, own, lists, surface_grads, surface_rows, ocean_start_grad.reshape(cells, channels), jnp.bfloat16
    ).reshape(row_count, col_count, channels)
    ocean_sums = weight_sums(ocean_record)
    atmos_sums = weight_sums(atmos_record)
    kernel_sums = full_sum(jnp.stack([atmos_record[4], ocean_record[4]])) / grad_scale
    return (
        atmos_next,
        ocean_next,
        atmos_state_grad,
        ocean_state_grad,
        atmos_sums[0],
        atmos_sums[1],
        kernel_sums[0],
        ocean_sums[0],
        ocean_sums[1],
        kernel_sums[1],
    )


def solution(mesh):
    return jax.shard_map(
        per_device,
        mesh=mesh,
        in_specs=(
            P("narrow", "wide", None),
            P("narrow", "wide", None),
            P("narrow", "wide"),
            P(),
            P(),
            P(),
            P(),
            P(),
            P(),
            P(),
            P(),
            P(),
            P(),
            P(),
            P(),
            P("narrow", "wide", None),
            P("narrow", "wide", None),
            P("narrow", "wide", None),
            P("narrow", "wide", None),
            P("narrow", "wide", None),
            P("narrow", "wide", None),
            P("narrow", "wide", None),
            P("narrow", "wide", None),
        ),
        out_specs=(
            P("narrow", "wide", None),
            P("narrow", "wide", None),
            P("narrow", "wide", None),
            P("narrow", "wide", None),
            P(("wide", "narrow"), None),
            P(("wide", "narrow"), None),
            P(),
            P(("wide", "narrow"), None),
            P(("wide", "narrow"), None),
            P(),
        ),
        check_vma=False,
    )
```

```python
import functools

import jax
import jax.numpy as jnp
from jax import lax
from jax.experimental import pallas as pl
from jax.experimental.pallas import tpu as pltpu
from jax.sharding import PartitionSpec as P

KERNEL = 7
TAPS = KERNEL * KERNEL
MARGIN = KERNEL // 2
LANES = 128
SIDE = 16

norm_eps = 1e-06
grad_scale = 256.0
highest = lax.Precision.HIGHEST


def pairs_along(axis, bit):
    return [(i, i ^ (1 << bit)) for i in range(lax.axis_size(axis))]


def bits_of(axis):
    return lax.axis_size(axis).bit_length() - 1


def stage_order(swapped):
    wide = [("wide", bit) for bit in range(bits_of("wide"))]
    narrow = [("narrow", bit) for bit in range(bits_of("narrow"))]
    return narrow[:1] + wide[:1] + narrow[1:] + wide[1:] if swapped else narrow + wide


def placed(order):
    labels = [("wide", bit) for bit in reversed(range(bits_of("wide")))]
    labels += [("narrow", bit) for bit in reversed(range(bits_of("narrow")))]
    bits = len(labels)
    places = []
    for block in range(1 << bits):
        place = 0
        for step in order:
            place = place * 2 + (block >> (bits - 1 - labels.index(step)) & 1)
        places.append(place)
    return places


def weight_grad_body(places, normed_ref, d_before_ref, hidden_ref, rounded_ref, *out_refs):
    chunk, width = pl.program_id(0), d_before_ref.shape[1]
    inner_ref = out_refs[0]
    together = len(out_refs) == 1
    blocks, channels = len(places[0]), normed_ref.shape[1]
    rows = channels // blocks
    columns = pl.ds(pl.multiple_of(chunk * width, width), width)
    over_cells = (((0,), (0,)), ((), ()))
    part = lax.dot_general(
        normed_ref[...], d_before_ref[...], over_cells, preferred_element_type=jnp.float32
    ).astype(jnp.bfloat16)
    for block, place in enumerate(places[0]):
        inner_ref[place, :rows, columns] = part[block * rows : (block + 1) * rows]
    part = lax.dot_general(
        hidden_ref[...], rounded_ref[...], over_cells, preferred_element_type=jnp.float32
    ).astype(jnp.bfloat16)
    tall = rows * d_before_ref.shape[1] * pl.num_programs(0) // channels
    here = width // tall
    for step in range(blocks // here):

        @pl.when(chunk == step)
        def _():
            for i in range(here):
                place = places[-1][step * here + i]
                piece = part[i * tall : (i + 1) * tall]
                if together:
                    for group in range(tall // rows):
                        inner_ref[place, rows:, group * channels : (group + 1) * channels] = piece[
                            group * rows : (group + 1) * rows
                        ]
                else:
                    out_refs[1][place] = piece


def weight_grads(normed, d_before, hidden, rounded, orders):
    cells, channels = normed.shape
    units = hidden.shape[1]
    blocks = lax.axis_size("wide") * lax.axis_size("narrow")
    rows = channels // blocks
    chunks = 4
    if len(orders) == 1:
        shapes = [(blocks, 2 * rows, units)]
    else:
        shapes = [(blocks, rows, units), (blocks, units // blocks, channels)]
    whole = lambda width: pl.BlockSpec((cells, width), lambda c: (0, 0))
    part = pl.BlockSpec((cells, units // chunks), lambda c: (0, c))
    return pl.pallas_call(
        functools.partial(weight_grad_body, [placed(order) for order in orders]),
        grid=(chunks,),
        in_specs=[whole(channels), part, part, whole(channels)],
        out_specs=[
            pl.BlockSpec(shape, lambda c: (0, 0, 0), pipeline_mode=pl.Buffered(1))
            for shape in shapes
        ],
        out_shape=[jax.ShapeDtypeStruct(shape, jnp.bfloat16) for shape in shapes],
        cost_estimate=pl.CostEstimate(flops=10**9, bytes_accessed=12 << 20, transcendentals=0),
        compiler_params=pltpu.CompilerParams(vmem_limit_bytes=24 << 20),
        name="weight_grads",
    )(normed, d_before, hidden, rounded)


def plain_weight_grads(normed, d_before, hidden, rounded, orders):
    blocks = lax.axis_size("wide") * lax.axis_size("narrow")
    parts = []
    for lhs, rhs, order in ((normed, d_before, orders[0]), (hidden, rounded, orders[-1])):
        part = lax.dot_general(
            lhs, rhs, (((0,), (0,)), ((), ())), preferred_element_type=jnp.float32
        ).astype(jnp.bfloat16)
        places = placed(order)
        back = [places.index(place) for place in range(blocks)]
        parts.append(part.reshape(blocks, -1, rhs.shape[1])[jnp.array(back)])
    return parts


class Sums:
    def __init__(self, together, normed, d_before, hidden, rounded):
        self.units, self.channels = hidden.shape[1], normed.shape[1]
        self.rows = self.channels // (lax.axis_size("wide") * lax.axis_size("narrow"))
        aligned = self.rows % 16 == 0
        self.together = together and aligned
        self.orders = [stage_order(False)] if self.together else [stage_order(False), stage_order(True)]
        make = weight_grads if aligned else plain_weight_grads
        self.parts = list(make(normed, d_before, hidden, rounded, self.orders))

    def step(self):
        for i, order in enumerate(self.orders):
            if not order:
                continue
            axis, bit = order.pop(0)
            count, rows, cols = self.parts[i].shape
            running = self.parts[i].reshape(2, count // 2, rows, cols)
            mine = (lax.axis_index(axis) >> bit) & 1
            keep = lax.dynamic_index_in_dim(running, mine, 0, keepdims=False)
            away = lax.dynamic_index_in_dim(running, 1 - mine, 0, keepdims=False)
            came = lax.ppermute(away, axis, pairs_along(axis, bit))
            running = keep.astype(jnp.float32) + came.astype(jnp.float32)
            self.parts[i] = running.astype(jnp.bfloat16) if order else running

    def hold(self, *chain):
        self.parts, chain = lax.optimization_barrier((self.parts, chain))
        return chain if len(chain) > 1 else chain[0]

    def result(self):
        while self.orders[0]:
            self.step()
        parts = [part[0] / grad_scale for part in self.parts]
        if self.together:
            inner, outer = parts[0][: self.rows], parts[0][self.rows :]
            outer = outer.reshape(self.rows, self.units // self.channels, self.channels)
            parts = [inner, outer.swapaxes(0, 1).reshape(-1, self.channels)]
        return parts


def doubling_sum(partial):
    for axis, bit in stage_order(False):
        partial = partial + lax.ppermute(partial, axis, pairs_along(axis, bit))
    return partial


def shift_pairs(axis, step, closed):
    count = lax.axis_size(axis)
    return [(i, (i + step) % count) for i in range(count) if closed or 0 <= i + step < count]


def from_sides(cells, axis, dim, width, closed):
    head = lax.slice_in_dim(cells, 0, width, axis=dim)
    tail = lax.slice_in_dim(cells, cells.shape[dim] - width, cells.shape[dim], axis=dim)
    return (
        lax.ppermute(tail, axis, shift_pairs(axis, 1, closed)),
        lax.ppermute(head, axis, shift_pairs(axis, -1, closed)),
    )


def normal_cdf(values):
    return 0.5 * (1.0 + lax.erf(values * 0.7071067811865476))


def normal_density(values):
    return jnp.exp(-0.5 * values * values) * 0.3989422804014327


def fold_band(beside):
    cols, rows = lax.axis_size("wide"), lax.axis_size("narrow")
    pairs = [(w * rows + rows - 1, (cols - 1 - w) * rows + rows - 1) for w in range(cols)]
    band = beside[beside.shape[0] - MARGIN :][::-1]
    length = band.shape[1]
    turn = jnp.arange(length)[:, None] + jnp.arange(length)[None, :] == length - 1
    turned = jnp.einsum(
        "ij,rjd->rid", turn.astype(band.dtype), band, preferred_element_type=jnp.float32
    ).astype(band.dtype)
    return lax.ppermute(turned, ("wide", "narrow"), pairs)


def roomy(padded):
    return jnp.pad(padded, ((0, 0), (0, SIDE - 2 * MARGIN), (0, 0)))


def extend(fields, folded, meanwhile):
    left, right = from_sides(fields, "wide", 1, MARGIN, True)
    left, right, _ = lax.optimization_barrier((left, right, meanwhile))
    beside = jnp.concatenate([left, fields, right], axis=1)
    below, above = from_sides(beside, "narrow", 0, MARGIN, False)
    mirror = fold_band(beside) if folded else None
    return jnp.concatenate([below, beside, above], axis=0), mirror


def spread_taps(kernel_ref, spread_ref, flipped):
    for tap in range(TAPS):
        place = TAPS - 1 - tap if flipped else tap
        row = kernel_ref[tap // KERNEL, pl.ds(tap % KERNEL, 1), :]
        spread_ref[place] = jnp.broadcast_to(row, spread_ref.shape[1:])


def convolve(wide_ref, first, spread_ref, out_ref):
    row_count, col_count, _ = out_ref.shape
    groups = (col_count // 8, 8, LANES)

    def one_row(row, sums, least, most):
        sums = list(sums)
        for b in range(KERNEL):
            cells = wide_ref[first + row, b : b + col_count, :].reshape(groups)
            for a in range(least, most):
                sums[a] = sums[a] + cells * spread_ref[a * KERNEL + b]
        return sums

    def finish(row, sums):
        out_ref[row - KERNEL + 1] = sums[-1].reshape(col_count, LANES)
        return [jnp.zeros(groups, jnp.float32), *sums[:-1]]

    sums = [jnp.zeros(groups, jnp.float32)] * KERNEL
    for row in range(KERNEL - 1):
        sums = one_row(row, sums, 0, row + 1)
        sums = [jnp.zeros(groups, jnp.float32), *sums[:-1]]

    def two_rows(pair, sums):
        for half in range(2):
            row = KERNEL - 1 + 2 * pair + half
            sums = finish(row, one_row(row, sums, 0, KERNEL))
        return tuple(sums)

    pairs = (row_count - KERNEL + 1) // 2
    sums = lax.fori_loop(0, pairs, two_rows, tuple(sums))
    for row in range(KERNEL - 1 + 2 * pairs, row_count + KERNEL - 1):
        sums = finish(row, one_row(row, sums, max(0, row - row_count + 1), KERNEL))


def conv_body(flipped, padded_ref, kernel_ref, out_ref, wide_ref, spread_ref):
    wide_ref[...] = padded_ref[...].astype(jnp.float32)
    spread_taps(kernel_ref, spread_ref, flipped)
    convolve(wide_ref, 0, spread_ref, out_ref)


def apply_kernel(padded, kernel, row_count, col_count, flipped):
    rows, cols, channels = padded.shape
    return pl.pallas_call(
        functools.partial(conv_body, flipped),
        grid=(channels // LANES,),
        in_specs=[
            pl.BlockSpec((rows, cols, LANES), lambda g: (0, 0, g)),
            pl.BlockSpec((KERNEL, KERNEL, LANES), lambda g: (0, 0, g)),
        ],
        out_specs=pl.BlockSpec((row_count, col_count, LANES), lambda g: (0, 0, g)),
        out_shape=jax.ShapeDtypeStruct((row_count, col_count, channels), jnp.float32),
        scratch_shapes=[
            pltpu.VMEM((rows, cols, LANES), jnp.float32),
            pltpu.VMEM((TAPS, 8, LANES), jnp.float32),
        ],
        cost_estimate=pl.CostEstimate(flops=10**9, bytes_accessed=3 << 20, transcendentals=0),
        compiler_params=pltpu.CompilerParams(vmem_limit_bytes=32 << 20),
        name="depthwise",
    )(padded, kernel)


def fold_body(band_ref, kernel_ref, out_ref, wide_ref):
    _, col_count, _ = out_ref.shape
    wide_ref[...] = band_ref[...].astype(jnp.float32)
    for row in range(MARGIN):
        total = jnp.zeros((col_count, LANES), jnp.float32)
        for band in range(row + 1):
            for b in range(KERNEL):
                tap = kernel_ref[KERNEL - 1 + band - row, pl.ds(b, 1), :]
                total = total + wide_ref[band, b : b + col_count, :] * tap
        out_ref[row] = total


def fold_taps(band, kernel, col_count):
    rows, cols, channels = band.shape
    return pl.pallas_call(
        fold_body,
        grid=(channels // LANES,),
        in_specs=[
            pl.BlockSpec((rows, cols, LANES), lambda g: (0, 0, g)),
            pl.BlockSpec((KERNEL, KERNEL, LANES), lambda g: (0, 0, g)),
        ],
        out_specs=pl.BlockSpec((rows, col_count, LANES), lambda g: (0, 0, g)),
        out_shape=jax.ShapeDtypeStruct((rows, col_count, channels), jnp.float32),
        scratch_shapes=[pltpu.VMEM((rows, cols, LANES), jnp.float32)],
        compiler_params=pltpu.CompilerParams(vmem_limit_bytes=32 << 20),
        name="fold_taps",
    )(band, kernel)


def kernel_grad_body(grad_ref, padded_ref, *refs):
    out_ref, wide_ref, tall_ref, sums_ref = refs[-4:]
    row_count, col_count, _ = grad_ref.shape
    groups = (col_count // 8, 8, LANES)
    wide_ref[...] = padded_ref[...].astype(jnp.float32)
    if len(refs) > 4:
        wide_ref[row_count + MARGIN :] += refs[0][...].astype(jnp.float32)
    tall_ref[...] = grad_ref[...].astype(jnp.float32)
    sums_ref[...] = jnp.zeros_like(sums_ref)

    def some_rows(first, count, pairs):
        grads = [tall_ref[first - KERNEL + 1 + i].reshape(groups) if i in pairs else None
                 for i in range(count + KERNEL - 1)]
        for b in range(KERNEL):
            cells = [wide_ref[first + i, b : b + col_count, :].reshape(groups) for i in range(count)]
            for a in range(KERNEL):
                terms = [
                    grads[i - a + KERNEL - 1] * cells[i]
                    for i in range(count)
                    if i - a + KERNEL - 1 in pairs
                ]
                if terms:
                    sums_ref[a * KERNEL + b] += jnp.sum(sum(terms[1:], terms[0]), axis=0)

    def main_rows(step, carry):
        some_rows(KERNEL - 1 + 2 * step, 2, range(KERNEL + 1))
        return carry

    steps = (row_count - KERNEL + 1) // 2
    for first in range(0, KERNEL - 1, 2):
        some_rows(first, 2, range(KERNEL - 1 - first, KERNEL + 1))
    lax.fori_loop(0, steps, main_rows, 0)
    for first in range(KERNEL - 1 + 2 * steps, row_count + KERNEL - 1, 2):
        some_rows(first, 2, range(0, row_count + KERNEL - 1 - first))
    out_ref[...] = jnp.sum(sums_ref[...], axis=1)


def kernel_grad(grads, padded, mirror=None):
    rows, cols, channels = padded.shape
    row_count, col_count, _ = grads.shape
    operands = [grads, padded] + ([] if mirror is None else [mirror])
    return pl.pallas_call(
        kernel_grad_body,
        grid=(channels // LANES,),
        in_specs=[pl.BlockSpec((*part.shape[:2], LANES), lambda g: (0, 0, g)) for part in operands],
        out_specs=pl.BlockSpec((TAPS, LANES), lambda g: (0, g)),
        out_shape=jax.ShapeDtypeStruct((TAPS, channels), jnp.float32),
        scratch_shapes=[
            pltpu.VMEM((rows, cols, LANES), jnp.float32),
            pltpu.VMEM((row_count, col_count, LANES), jnp.float32),
            pltpu.VMEM((TAPS, 8, LANES), jnp.float32),
        ],
        cost_estimate=pl.CostEstimate(flops=10**9, bytes_accessed=3 << 20, transcendentals=0),
        compiler_params=pltpu.CompilerParams(vmem_limit_bytes=32 << 20),
        name="kernel_grad",
    )(*operands)


def add_last_rows(values, rows):
    return values + jnp.pad(rows, ((values.shape[0] - rows.shape[0], 0), (0, 0), (0, 0)))


def block_forward(
    padded, mixed_taps, mirror, start_field, kernel, norm_gain, inner_weight, outer_weight
):
    row_count, col_count, channels = start_field.shape
    if mirror is not None:
        mixed_taps = add_last_rows(mixed_taps, fold_taps(mirror, kernel, col_count))
    center = mixed_taps - jnp.mean(mixed_taps, axis=-1, keepdims=True)
    inverse = lax.rsqrt(jnp.mean(center * center, axis=-1, keepdims=True) + norm_eps)
    scaled = center * inverse
    normed = (scaled * norm_gain).astype(jnp.bfloat16).reshape(-1, channels)
    before = jnp.dot(normed, inner_weight, preferred_element_type=jnp.float32)
    hidden = (before * normal_cdf(before)).astype(jnp.bfloat16)
    branch = jnp.dot(hidden, outer_weight, preferred_element_type=jnp.float32).reshape(
        row_count, col_count, channels
    )
    return (branch, (padded, scaled, inverse, normed, before, hidden))


def block_backward(stored, norm_gain, inner_weight, outer_weight, incoming, together):
    _, scaled, inverse, normed, before, hidden = stored
    row_count, col_count, channels = scaled.shape
    rounded = incoming.astype(jnp.bfloat16).reshape(-1, channels)
    d_hidden = jnp.einsum("cd,fd->cf", rounded, outer_weight, preferred_element_type=jnp.float32)
    slopes = normal_cdf(before) + before * normal_density(before)
    d_before = (d_hidden * slopes).astype(jnp.bfloat16)
    sums = Sums(together, normed, d_before, hidden, rounded)
    sums.step()
    d_normed = jnp.einsum("cf,df->cd", d_before, inner_weight, preferred_element_type=jnp.float32)
    d_scaled = d_normed.reshape(row_count, col_count, channels) * norm_gain
    mean_grad = jnp.mean(d_scaled, axis=-1, keepdims=True)
    mean_cross = jnp.mean(d_scaled * scaled, axis=-1, keepdims=True)
    d_taps = (inverse * (d_scaled - mean_grad - scaled * mean_cross)).astype(jnp.bfloat16)
    return d_taps, sums


def in_column(tile):
    return lax.all_gather(tile, "narrow", axis=0, tiled=False)


def around(tile, reach):
    return beside_column(in_column(tile), reach)


def beside_column(column, reach):
    return [
        lax.ppermute(column, "wide", shift_pairs("wide", -offset, True)) if offset else column
        for offset in range(-reach, reach + 1)
    ]


def across(lhs, rhs):
    return lax.dot_general(lhs, rhs, (((1,), (1,)), ((), ())), preferred_element_type=jnp.float32)


def three_parts(values):
    parts = []
    for _ in range(3):
        part = values.astype(jnp.bfloat16)
        parts.append(part)
        values = values - part.astype(jnp.float32)
    return jnp.concatenate([part.astype(jnp.float32) for part in parts]).astype(jnp.bfloat16)


def summed(stacked):
    count = stacked.shape[0] // 3
    return stacked[:count] + stacked[count : 2 * count] + stacked[2 * count :]


def head_body(with_lists, state_ref, head_ref, *refs):
    out_ref = refs[-1]
    blocks = state_ref.shape[0] // LANES
    fields = head_ref.shape[0]
    rows = [
        across(head_ref[...], state_ref[pl.ds(block * LANES, LANES), :]) for block in range(blocks)
    ]
    if with_lists:
        for first in (0, 3):
            lists = [ref[0].astype(jnp.float32) for ref in refs[first : first + 3]]
            gap = jnp.zeros((1, LANES - lists[0].shape[1]), jnp.float32)
            sources, targets, weights = (jnp.concatenate([part, gap], axis=1) for part in lists)
            rows += [sources, targets, three_parts(weights).astype(jnp.float32)]
        rows.append(jnp.zeros((out_ref.shape[0] - blocks * fields - 10, LANES), jnp.float32))
    out_ref[...] = jnp.concatenate(rows).astype(jnp.bfloat16)


def coupled_fields(state, head_rows, lists=()):
    cells, channels = state.shape
    rows = cells // LANES * head_rows.shape[0] + (16 if lists else 0)
    operands = [state, head_rows, *lists]
    return pl.pallas_call(
        functools.partial(head_body, bool(lists)),
        out_shape=jax.ShapeDtypeStruct((rows, LANES), jnp.bfloat16),
        compiler_params=pltpu.CompilerParams(vmem_limit_bytes=32 << 20),
        name="coupled_fields",
    )(*operands)


def list_of(lists_ref, tile, which, first):
    rows = lists_ref[tile, first:, :].astype(jnp.float32)[5 * which : 5 * which + 5]
    return rows[0:1].astype(jnp.int32), rows[1:2].astype(jnp.int32), [rows[i : i + 1] for i in (2, 3, 4)]


def rows_like(index, parts, count):
    at = lax.broadcasted_iota(jnp.int32, (count, LANES), 0) == index
    return jnp.concatenate([jnp.where(at, part, 0.0) for part in parts]).astype(jnp.bfloat16)


def chosen(index):
    at = lax.broadcasted_iota(jnp.int32, (LANES, LANES), 0) == index
    return jnp.where(at, 1.0, 0.0).astype(jnp.bfloat16)


def remap_blocks(matrix, blocks_refs, cells_ref, sums_ref, fields, used):
    cells_ref[...] = jnp.zeros_like(cells_ref)
    lat_count = blocks_refs[0].shape[0]
    for i, ref in enumerate(blocks_refs):
        for tile in range(lat_count):
            cells_ref[pl.ds((i * lat_count + tile) * used, used), :] = ref[tile, :used, :].astype(jnp.float32)
    parts = three_parts(matrix)
    for k in range(fields):
        blocks = cells_ref[pl.ds(k, LANES, stride=fields), :].astype(jnp.bfloat16)
        mixed = jnp.dot(parts, blocks, preferred_element_type=jnp.float32)
        sums_ref[pl.ds(k, matrix.shape[0], stride=fields), :] = summed(mixed)


def lift_block(sums, weights):
    parts = three_parts(sums)
    return lax.dot_general(
        parts,
        jnp.concatenate([weights.astype(jnp.float32)] * 3).astype(jnp.bfloat16),
        (((0,), (0,)), ((), ())),
        preferred_element_type=jnp.float32,
    )


def start_body(which, masked, own_ref, *refs):
    lists, blocks = refs[:3], refs[3:8]
    state_ref, left_ref, right_ref, below_ref, above_ref, lift_ref, kernel_ref = refs[8:15]
    padded_ref, start_ref, taps_ref = refs[15:18]
    cells_ref, sums_ref, block_ref, wide_ref, spread_ref, wet_ref = refs[18:]
    lat_count = blocks[0].shape[0]
    row_count, col_count, _ = taps_ref.shape
    fields = lift_ref.shape[0]
    block_rows = LANES // col_count
    count = row_count // block_rows
    used = count * fields
    extra = block_rows - MARGIN
    own = own_ref[0]

    @pl.when(pl.program_id(0) == 0)
    def _():
        matrix = []
        for column in range(3):
            mixed = jnp.zeros((3 * (count + 2), LANES), jnp.float32)
            for beside in (-1, 0, 1):
                tile = own + beside
                inside = jnp.where((tile >= 0) & (tile < lat_count), 1.0, 0.0)
                sources, targets, parts = list_of(
                    lists[column], jnp.clip(tile, 0, lat_count - 1), which, used
                )
                placing = rows_like(
                    targets + 1 + beside * count, [part * inside for part in parts], count + 2
                )
                mixed = mixed + across(placing, chosen(sources + column * lat_count * count))
            matrix.append(summed(mixed))
        remap_blocks(jnp.concatenate(matrix), blocks, cells_ref, sums_ref, fields, used)

    wide_ref[...] = jnp.zeros_like(wide_ref)
    left, right = col_count + MARGIN, col_count + 2 * MARGIN
    rows = slice(extra, extra + row_count + 2 * MARGIN)
    inner = slice(extra + MARGIN, extra + MARGIN + row_count)
    top = slice(extra + MARGIN + row_count, extra + row_count + 2 * MARGIN)
    wide_ref[inner, 0:MARGIN, :] = left_ref[...].astype(jnp.float32)
    wide_ref[inner, MARGIN:left, :] = state_ref[...].astype(jnp.float32)
    wide_ref[inner, left:right, :] = right_ref[...].astype(jnp.float32)
    wide_ref[extra : extra + MARGIN, 0:right, :] = below_ref[...].astype(jnp.float32)
    wide_ref[top, 0:right, :] = above_ref[...].astype(jnp.float32)
    if masked:

        @pl.when(pl.program_id(0) == 0)
        def _():
            wet = jnp.where(wide_ref[rows, :, 0:1] < 100.0, 1.0, 0.0)
            wet_ref[...] = jnp.broadcast_to(wet, wet_ref.shape)

    for column in range(3):
        for block in range(count + 2):
            sums = sums_ref[pl.ds((column * (count + 2) + block) * fields, fields), :]
            block_ref[...] = lift_block(sums, lift_ref[...]).reshape(block_ref.shape)
            here = slice(block * block_rows, (block + 1) * block_rows)
            if column == 0:
                wide_ref[here, 0:MARGIN, :] += block_ref[:, col_count - MARGIN : col_count, :]
            elif column == 1:
                wide_ref[here, MARGIN:left, :] += block_ref[...]
            else:
                wide_ref[here, left:right, :] += block_ref[:, 0:MARGIN, :]
    start = wide_ref[rows]
    if masked:
        start = jnp.where(wet_ref[...] > 0.5, start, 0.0)
    start = start.astype(jnp.bfloat16)
    padded_ref[...] = start
    wide_ref[rows] = start.astype(jnp.float32)
    start_ref[...] = wide_ref[inner, MARGIN:left, :].astype(jnp.bfloat16)
    spread_taps(kernel_ref, spread_ref, False)
    convolve(wide_ref, extra, spread_ref, taps_ref)


def start_and_taps(which, masked, own, lists, blocks, states, lift_weight, kernel):
    row_count, col_count, channels = states[0].shape[1:]
    rows, cols = row_count + 2 * MARGIN, col_count + SIDE
    grid_index = 1 if masked else 0
    fields = lift_weight.shape[0]
    block_rows = LANES // col_count
    count = row_count // block_rows + 2
    whole = lambda part: pl.BlockSpec(part.shape, lambda g: (0, 0, 0))
    piece = lambda part: pl.BlockSpec((None, *part.shape[1:3], LANES), lambda g: (grid_index, 0, 0, g))
    return pl.pallas_call(
        functools.partial(start_body, which, masked),
        grid=(channels // LANES,),
        in_specs=[
            pl.BlockSpec(memory_space=pltpu.SMEM),
            *[whole(part) for part in lists],
            *[whole(part) for part in blocks],
            *[piece(part) for part in states],
            pl.BlockSpec((fields, LANES), lambda g: (0, g)),
            pl.BlockSpec((KERNEL, KERNEL, LANES), lambda g: (0, 0, g)),
        ],
        out_specs=[
            pl.BlockSpec((rows, cols, LANES), lambda g: (0, 0, g)),
            pl.BlockSpec((row_count, col_count, LANES), lambda g: (0, 0, g)),
            pl.BlockSpec((row_count, col_count, LANES), lambda g: (0, 0, g)),
        ],
        out_shape=[
            jax.ShapeDtypeStruct((rows, cols, channels), jnp.bfloat16),
            jax.ShapeDtypeStruct((row_count, col_count, channels), jnp.bfloat16),
            jax.ShapeDtypeStruct((row_count, col_count, channels), jnp.float32),
        ],
        scratch_shapes=[
            pltpu.VMEM((LANES * fields, LANES), jnp.float32),
            pltpu.VMEM((3 * count * fields, LANES), jnp.float32),
            pltpu.VMEM((block_rows, col_count, LANES), jnp.float32),
            pltpu.VMEM((count * block_rows, cols, LANES), jnp.float32),
            pltpu.VMEM((TAPS, 8, LANES), jnp.float32),
            pltpu.VMEM((rows, cols, LANES), jnp.float32),
        ],
        cost_estimate=pl.CostEstimate(flops=10**9, bytes_accessed=3 << 20, transcendentals=0),
        compiler_params=pltpu.CompilerParams(vmem_limit_bytes=56 << 20),
        name="start_and_taps",
    )(own, *lists, *blocks, *states, lift_weight, kernel)


def total_body(which, first, own_ref, *refs):
    lists, blocks = refs[:3], refs[3:6]
    head_ref, base_ref, out_ref, cells_ref, sums_ref = refs[6:]
    lat_count = blocks[0].shape[0]
    fields = head_ref.shape[0]
    count = base_ref.shape[0] // LANES
    own = own_ref[0]
    mixed = jnp.zeros((24, LANES), jnp.float32)
    for column in range(3):
        for tile in range(lat_count):
            sources, targets, parts = list_of(lists[column], tile, which, first)
            local = sources - ((2 - column) * lat_count + own) * count
            local = jnp.where(local < count, local, -1)
            place = chosen(targets + (column * lat_count + tile) * count)
            mixed = mixed + across(rows_like(local, parts, 8), place)
    remap_blocks(summed(mixed), blocks, cells_ref, sums_ref, fields, count * fields)
    for block in range(count):
        rows = pl.ds(block * LANES, LANES)
        back = lift_block(sums_ref[pl.ds(block * fields, fields), :], head_ref[...])
        out_ref[rows, :] = (base_ref[rows, :].astype(jnp.float32) + back).astype(out_ref.dtype)


def add_remap_adjoint(which, own, lists, blocks, head_rows, base, kind):
    fields = head_rows.shape[0]
    first = base.shape[0] // LANES * fields
    memory = pl.BlockSpec(memory_space=pltpu.VMEM)
    return pl.pallas_call(
        functools.partial(total_body, which, first),
        in_specs=[pl.BlockSpec(memory_space=pltpu.SMEM)] + [memory] * 8,
        out_shape=jax.ShapeDtypeStruct(base.shape, kind),
        scratch_shapes=[
            pltpu.VMEM((LANES * fields, LANES), jnp.float32),
            pltpu.VMEM((8 * fields, LANES), jnp.float32),
        ],
        compiler_params=pltpu.CompilerParams(vmem_limit_bytes=32 << 20),
        name="add_remap_adjoint",
    )(own, *lists, *blocks, head_rows, base)


def side_strips(states):
    size = states.shape[2]
    return (
        lax.ppermute(states[:, :, size - MARGIN :], "wide", shift_pairs("wide", 1, True)),
        lax.ppermute(states[:, :, :MARGIN], "wide", shift_pairs("wide", -1, True)),
    )


def end_strips(states, left, right):
    def across_columns(rows):
        return jnp.concatenate([left[:, rows], states[:, rows], right[:, rows]], axis=2)

    size = states.shape[1]
    return (
        lax.ppermute(across_columns(slice(size - MARGIN, size)), "narrow", shift_pairs("narrow", 1, False)),
        lax.ppermute(across_columns(slice(0, MARGIN)), "narrow", shift_pairs("narrow", -1, False)),
    )


def lift_back(gradient, lift_weight):
    return jnp.einsum(
        "bpd,kd->bkp",
        gradient.reshape(-1, 128, lift_weight.shape[1]),
        lift_weight.astype(jnp.float32),
        precision=highest,
    )


def per_device(
    atmos_state,
    ocean_state,
    wet_mask,
    atmos_kernel,
    atmos_gain,
    atmos_inner,
    atmos_outer,
    ocean_kernel,
    ocean_gain,
    ocean_inner,
    ocean_outer,
    flux_head,
    flux_lift,
    surface_head,
    surface_lift,
    flux_source,
    flux_target,
    flux_weight,
    surface_source,
    surface_target,
    surface_weight,
    atmos_cotangent,
    ocean_cotangent,
):
    row_count, col_count, channels = atmos_state.shape
    wet_cells = wet_mask.astype(jnp.float32)[:, :, None]
    own = lax.axis_index("narrow").reshape(1).astype(jnp.int32)
    lists = [flux_source, flux_target, flux_weight, surface_source, surface_target, surface_weight]
    flux_rows, surface_rows = flux_head.T, surface_head.T
    cells = row_count * col_count
    marked = jnp.where(wet_mask[:, :, None] > 0, ocean_state, jnp.bfloat16(1024.0))
    states = jnp.stack([atmos_state, marked])
    left, right = side_strips(states)
    column = in_column(coupled_fields(ocean_state.reshape(cells, channels), surface_rows, lists))
    column, left, right = lax.optimization_barrier((column, left, right))
    states = (states, left, right, *end_strips(states, left, right))
    first = beside_column(column, 2)
    lists = first[1:4]
    atmos_padded, atmos_start, atmos_taps = start_and_taps(
        1, False, own, lists, first, states, surface_lift, atmos_kernel
    )
    atmos_branch, atmos_stored = block_forward(
        atmos_padded, atmos_taps, None, atmos_start, atmos_kernel, atmos_gain, atmos_inner, atmos_outer
    )
    atmos_next = (atmos_start + atmos_branch).astype(jnp.bfloat16)
    fluxes = around(coupled_fields(atmos_next.reshape(cells, channels), flux_rows), 2)
    ocean_padded, ocean_start, ocean_taps = start_and_taps(
        0, True, own, lists, fluxes, states, flux_lift, ocean_kernel
    )
    own_rows = slice(MARGIN, MARGIN + row_count)
    mirror = roomy(fold_band(ocean_padded[own_rows, : col_count + 2 * MARGIN]))
    ocean_branch, ocean_stored = block_forward(
        ocean_padded, ocean_taps, mirror, ocean_start, ocean_kernel, ocean_gain, ocean_inner, ocean_outer
    )
    ocean_next = ((ocean_start + ocean_branch) * wet_cells).astype(jnp.bfloat16)
    ocean_total = ocean_cotangent * wet_cells
    ocean_d_taps, ocean_sums = block_backward(
        ocean_stored, ocean_gain, ocean_inner, ocean_outer, ocean_total, True
    )
    ocean_kernel_part = kernel_grad(ocean_d_taps, ocean_stored[0], mirror)
    grad_padded, grad_mirror = extend(ocean_d_taps, True, ocean_kernel_part)
    spread = apply_kernel(roomy(grad_padded), ocean_kernel, row_count, col_count, True)
    fold_part = fold_taps(roomy(grad_mirror), ocean_kernel, col_count)
    spread = add_last_rows(spread, fold_part)
    ocean_start_grad = (ocean_total + spread) * wet_cells
    flux_grads = lift_back(ocean_start_grad, flux_lift).astype(jnp.bfloat16)
    flux_grads = around(flux_grads.reshape(-1, LANES), 1)
    flux_grads = ocean_sums.hold(*flux_grads)
    ocean_sums.step()
    atmos_total = add_remap_adjoint(
        0, own, lists, flux_grads, flux_rows, atmos_cotangent.reshape(cells, channels), jnp.float32
    ).reshape(row_count, col_count, channels)
    atmos_d_taps, atmos_sums = block_backward(
        atmos_stored, atmos_gain, atmos_inner, atmos_outer, atmos_total, False
    )
    atmos_d_taps = ocean_sums.hold(atmos_d_taps)
    ocean_sums.step()
    atmos_d_taps = atmos_sums.hold(atmos_d_taps)
    atmos_sums.step()
    atmos_kernel_part = kernel_grad(atmos_d_taps, atmos_stored[0])
    grad_padded, _ = extend(atmos_d_taps, False, atmos_kernel_part)
    grad_padded = ocean_sums.hold(grad_padded)
    ocean_sums.step()
    spread = apply_kernel(roomy(grad_padded), atmos_kernel, row_count, col_count, True)
    atmos_start_grad = atmos_total + spread
    atmos_state_grad = atmos_start_grad.astype(jnp.bfloat16)
    surface_grads = lift_back(atmos_start_grad, surface_lift).astype(jnp.bfloat16)
    surface_grads = around(surface_grads.reshape(-1, LANES), 1)
    ocean_state_grad = add_remap_adjoint(
        1, own, lists, surface_grads, surface_rows, ocean_start_grad.reshape(cells, channels), jnp.bfloat16
    ).reshape(row_count, col_count, channels)
    ocean_sums, atmos_sums = ocean_sums.result(), atmos_sums.result()
    kernel_sums = doubling_sum(jnp.stack([atmos_kernel_part, ocean_kernel_part])) / grad_scale
    kernel_sums = kernel_sums.reshape(2, KERNEL, KERNEL, channels)
    return (
        atmos_next,
        ocean_next,
        atmos_state_grad,
        ocean_state_grad,
        atmos_sums[0],
        atmos_sums[1],
        kernel_sums[0],
        ocean_sums[0],
        ocean_sums[1],
        kernel_sums[1],
    )


def solution(mesh):
    return jax.shard_map(
        per_device,
        mesh=mesh,
        in_specs=(
            P("narrow", "wide", None),
            P("narrow", "wide", None),
            P("narrow", "wide"),
            P(),
            P(),
            P(),
            P(),
            P(),
            P(),
            P(),
            P(),
            P(),
            P(),
            P(),
            P(),
            P("narrow", "wide", None),
            P("narrow", "wide", None),
            P("narrow", "wide", None),
            P("narrow", "wide", None),
            P("narrow", "wide", None),
            P("narrow", "wide", None),
            P("narrow", "wide", None),
            P("narrow", "wide", None),
        ),
        out_specs=(
            P("narrow", "wide", None),
            P("narrow", "wide", None),
            P("narrow", "wide", None),
            P("narrow", "wide", None),
            P(("wide", "narrow"), None),
            P(("wide", "narrow"), None),
            P(),
            P(("wide", "narrow"), None),
            P(("wide", "narrow"), None),
            P(),
        ),
        check_vma=False,
    )
```

```python
import functools

import jax
import jax.numpy as jnp
from jax import lax
from jax.experimental import pallas as pl
from jax.experimental.pallas import tpu as pltpu
from jax.sharding import PartitionSpec as P

KERNEL = 7
TAPS = KERNEL * KERNEL
MARGIN = KERNEL // 2
LANES = 128
SIDE = 16

norm_eps = 1e-06
grad_scale = 256.0
highest = lax.Precision.HIGHEST


def pairs_along(axis, bit):
    return [(i, i ^ (1 << bit)) for i in range(lax.axis_size(axis))]


def bits_of(axis):
    return lax.axis_size(axis).bit_length() - 1


def stage_order(swapped):
    wide = [("wide", bit) for bit in range(bits_of("wide"))]
    narrow = [("narrow", bit) for bit in range(bits_of("narrow"))]
    return narrow[:1] + wide[:1] + narrow[1:] + wide[1:] if swapped else narrow + wide


def placed(order):
    labels = [("wide", bit) for bit in reversed(range(bits_of("wide")))]
    labels += [("narrow", bit) for bit in reversed(range(bits_of("narrow")))]
    bits = len(labels)
    places = []
    for block in range(1 << bits):
        place = 0
        for step in order:
            place = place * 2 + (block >> (bits - 1 - labels.index(step)) & 1)
        places.append(place)
    return places


def weight_grad_body(places, normed_ref, d_before_ref, hidden_ref, rounded_ref, *out_refs):
    chunk, width = pl.program_id(0), d_before_ref.shape[1]
    inner_ref = out_refs[0]
    together = len(out_refs) == 1
    blocks, channels = len(places[0]), normed_ref.shape[1]
    rows = channels // blocks
    columns = pl.ds(pl.multiple_of(chunk * width, width), width)
    over_cells = (((0,), (0,)), ((), ()))
    part = lax.dot_general(
        normed_ref[...], d_before_ref[...], over_cells, preferred_element_type=jnp.float32
    ).astype(jnp.bfloat16)
    for block, place in enumerate(places[0]):
        inner_ref[place, :rows, columns] = part[block * rows : (block + 1) * rows]
    part = lax.dot_general(
        hidden_ref[...], rounded_ref[...], over_cells, preferred_element_type=jnp.float32
    ).astype(jnp.bfloat16)
    tall = rows * d_before_ref.shape[1] * pl.num_programs(0) // channels
    here = width // tall
    for step in range(blocks // here):

        @pl.when(chunk == step)
        def _():
            for i in range(here):
                place = places[-1][step * here + i]
                piece = part[i * tall : (i + 1) * tall]
                if together:
                    for group in range(tall // rows):
                        inner_ref[place, rows:, group * channels : (group + 1) * channels] = piece[
                            group * rows : (group + 1) * rows
                        ]
                else:
                    out_refs[1][place] = piece


def weight_grads(normed, d_before, hidden, rounded, orders):
    cells, channels = normed.shape
    units = hidden.shape[1]
    blocks = lax.axis_size("wide") * lax.axis_size("narrow")
    rows = channels // blocks
    chunks = 4
    if len(orders) == 1:
        shapes = [(blocks, 2 * rows, units)]
    else:
        shapes = [(blocks, rows, units), (blocks, units // blocks, channels)]
    whole = lambda width: pl.BlockSpec((cells, width), lambda c: (0, 0))
    part = pl.BlockSpec((cells, units // chunks), lambda c: (0, c))
    return pl.pallas_call(
        functools.partial(weight_grad_body, [placed(order) for order in orders]),
        grid=(chunks,),
        in_specs=[whole(channels), part, part, whole(channels)],
        out_specs=[
            pl.BlockSpec(shape, lambda c: (0, 0, 0), pipeline_mode=pl.Buffered(1))
            for shape in shapes
        ],
        out_shape=[jax.ShapeDtypeStruct(shape, jnp.bfloat16) for shape in shapes],
        cost_estimate=pl.CostEstimate(flops=10**9, bytes_accessed=12 << 20, transcendentals=0),
        compiler_params=pltpu.CompilerParams(vmem_limit_bytes=24 << 20),
        name="weight_grads",
    )(normed, d_before, hidden, rounded)


def plain_weight_grads(normed, d_before, hidden, rounded, orders):
    blocks = lax.axis_size("wide") * lax.axis_size("narrow")
    parts = []
    for lhs, rhs, order in ((normed, d_before, orders[0]), (hidden, rounded, orders[-1])):
        part = lax.dot_general(
            lhs, rhs, (((0,), (0,)), ((), ())), preferred_element_type=jnp.float32
        ).astype(jnp.bfloat16)
        places = placed(order)
        back = [places.index(place) for place in range(blocks)]
        parts.append(part.reshape(blocks, -1, rhs.shape[1])[jnp.array(back)])
    return parts


class Sums:
    def __init__(self, together, normed, d_before, hidden, rounded):
        self.units, self.channels = hidden.shape[1], normed.shape[1]
        self.rows = self.channels // (lax.axis_size("wide") * lax.axis_size("narrow"))
        aligned = self.rows % 16 == 0
        self.together = together and aligned
        self.orders = [stage_order(False)] if self.together else [stage_order(False), stage_order(True)]
        make = weight_grads if aligned else plain_weight_grads
        self.parts = list(make(normed, d_before, hidden, rounded, self.orders))

    def step(self):
        for i, order in enumerate(self.orders):
            if not order:
                continue
            axis, bit = order.pop(0)
            count, rows, cols = self.parts[i].shape
            running = self.parts[i].reshape(2, count // 2, rows, cols)
            mine = (lax.axis_index(axis) >> bit) & 1
            keep = lax.dynamic_index_in_dim(running, mine, 0, keepdims=False)
            away = lax.dynamic_index_in_dim(running, 1 - mine, 0, keepdims=False)
            came = lax.ppermute(away, axis, pairs_along(axis, bit))
            running = keep.astype(jnp.float32) + came.astype(jnp.float32)
            self.parts[i] = running.astype(jnp.bfloat16) if order else running

    def hold(self, *chain):
        self.parts, chain = lax.optimization_barrier((self.parts, chain))
        return chain if len(chain) > 1 else chain[0]

    def result(self):
        while self.orders[0]:
            self.step()
        parts = [part[0] / grad_scale for part in self.parts]
        if self.together:
            inner, outer = parts[0][: self.rows], parts[0][self.rows :]
            outer = outer.reshape(self.rows, self.units // self.channels, self.channels)
            parts = [inner, outer.swapaxes(0, 1).reshape(-1, self.channels)]
        return parts


def doubling_sum(partial):
    for axis, bit in stage_order(False):
        partial = partial + lax.ppermute(partial, axis, pairs_along(axis, bit))
    return partial


def shift_pairs(axis, step, closed):
    count = lax.axis_size(axis)
    return [(i, (i + step) % count) for i in range(count) if closed or 0 <= i + step < count]


def from_sides(cells, axis, dim, width, closed):
    head = lax.slice_in_dim(cells, 0, width, axis=dim)
    tail = lax.slice_in_dim(cells, cells.shape[dim] - width, cells.shape[dim], axis=dim)
    return (
        lax.ppermute(tail, axis, shift_pairs(axis, 1, closed)),
        lax.ppermute(head, axis, shift_pairs(axis, -1, closed)),
    )


def normal_cdf(values):
    return 0.5 * (1.0 + lax.erf(values * 0.7071067811865476))


def normal_density(values):
    return jnp.exp(-0.5 * values * values) * 0.3989422804014327


def fold_band(beside):
    cols, rows = lax.axis_size("wide"), lax.axis_size("narrow")
    pairs = [(w * rows + rows - 1, (cols - 1 - w) * rows + rows - 1) for w in range(cols)]
    band = beside[beside.shape[0] - MARGIN :][::-1]
    length = band.shape[1]
    turn = jnp.arange(length)[:, None] + jnp.arange(length)[None, :] == length - 1
    turned = jnp.einsum(
        "ij,rjd->rid", turn.astype(band.dtype), band, preferred_element_type=jnp.float32
    ).astype(band.dtype)
    return lax.ppermute(turned, ("wide", "narrow"), pairs)


def roomy(padded):
    return jnp.pad(padded, ((0, 0), (0, SIDE - 2 * MARGIN), (0, 0)))


def extend(fields, folded, meanwhile):
    left, right = from_sides(fields, "wide", 1, MARGIN, True)
    left, right, _ = lax.optimization_barrier((left, right, meanwhile))
    beside = jnp.concatenate([left, fields, right], axis=1)
    below, above = from_sides(beside, "narrow", 0, MARGIN, False)
    mirror = fold_band(beside) if folded else None
    return jnp.concatenate([below, beside, above], axis=0), mirror


def spread_taps(kernel_ref, spread_ref, flipped):
    for tap in range(TAPS):
        place = TAPS - 1 - tap if flipped else tap
        row = kernel_ref[tap // KERNEL, pl.ds(tap % KERNEL, 1), :]
        spread_ref[place] = jnp.broadcast_to(row, spread_ref.shape[1:])


def convolve(wide_ref, first, spread_ref, out_ref):
    row_count, col_count, _ = out_ref.shape
    groups = (col_count // 8, 8, LANES)

    def one_row(row, sums, least, most):
        sums = list(sums)
        for b in range(KERNEL):
            cells = wide_ref[first + row, b : b + col_count, :].reshape(groups)
            for a in range(least, most):
                sums[a] = sums[a] + cells * spread_ref[a * KERNEL + b]
        return sums

    def finish(row, sums):
        out_ref[row - KERNEL + 1] = sums[-1].reshape(col_count, LANES)
        return [jnp.zeros(groups, jnp.float32), *sums[:-1]]

    sums = [jnp.zeros(groups, jnp.float32)] * KERNEL
    for row in range(KERNEL - 1):
        sums = one_row(row, sums, 0, row + 1)
        sums = [jnp.zeros(groups, jnp.float32), *sums[:-1]]

    def two_rows(pair, sums):
        for half in range(2):
            row = KERNEL - 1 + 2 * pair + half
            sums = finish(row, one_row(row, sums, 0, KERNEL))
        return tuple(sums)

    pairs = (row_count - KERNEL + 1) // 2
    sums = lax.fori_loop(0, pairs, two_rows, tuple(sums))
    for row in range(KERNEL - 1 + 2 * pairs, row_count + KERNEL - 1):
        sums = finish(row, one_row(row, sums, max(0, row - row_count + 1), KERNEL))


def conv_body(flipped, padded_ref, kernel_ref, out_ref, wide_ref, spread_ref):
    wide_ref[...] = padded_ref[...].astype(jnp.float32)
    spread_taps(kernel_ref, spread_ref, flipped)
    convolve(wide_ref, 0, spread_ref, out_ref)


def apply_kernel(padded, kernel, row_count, col_count, flipped):
    rows, cols, channels = padded.shape
    return pl.pallas_call(
        functools.partial(conv_body, flipped),
        grid=(channels // LANES,),
        in_specs=[
            pl.BlockSpec((rows, cols, LANES), lambda g: (0, 0, g)),
            pl.BlockSpec((KERNEL, KERNEL, LANES), lambda g: (0, 0, g)),
        ],
        out_specs=pl.BlockSpec((row_count, col_count, LANES), lambda g: (0, 0, g)),
        out_shape=jax.ShapeDtypeStruct((row_count, col_count, channels), jnp.float32),
        scratch_shapes=[
            pltpu.VMEM((rows, cols, LANES), jnp.float32),
            pltpu.VMEM((TAPS, 8, LANES), jnp.float32),
        ],
        cost_estimate=pl.CostEstimate(flops=10**9, bytes_accessed=3 << 20, transcendentals=0),
        compiler_params=pltpu.CompilerParams(vmem_limit_bytes=32 << 20),
        name="depthwise",
    )(padded, kernel)


def fold_body(band_ref, kernel_ref, out_ref, wide_ref):
    _, col_count, _ = out_ref.shape
    wide_ref[...] = band_ref[...].astype(jnp.float32)
    for row in range(MARGIN):
        total = jnp.zeros((col_count, LANES), jnp.float32)
        for band in range(row + 1):
            for b in range(KERNEL):
                tap = kernel_ref[KERNEL - 1 + band - row, pl.ds(b, 1), :]
                total = total + wide_ref[band, b : b + col_count, :] * tap
        out_ref[row] = total


def fold_taps(band, kernel, col_count):
    rows, cols, channels = band.shape
    return pl.pallas_call(
        fold_body,
        grid=(channels // LANES,),
        in_specs=[
            pl.BlockSpec((rows, cols, LANES), lambda g: (0, 0, g)),
            pl.BlockSpec((KERNEL, KERNEL, LANES), lambda g: (0, 0, g)),
        ],
        out_specs=pl.BlockSpec((rows, col_count, LANES), lambda g: (0, 0, g)),
        out_shape=jax.ShapeDtypeStruct((rows, col_count, channels), jnp.float32),
        scratch_shapes=[pltpu.VMEM((rows, cols, LANES), jnp.float32)],
        compiler_params=pltpu.CompilerParams(vmem_limit_bytes=32 << 20),
        name="fold_taps",
    )(band, kernel)


def kernel_grad_body(grad_ref, padded_ref, *refs):
    out_ref, wide_ref, tall_ref, sums_ref = refs[-4:]
    row_count, col_count, _ = grad_ref.shape
    groups = (col_count // 8, 8, LANES)
    wide_ref[...] = padded_ref[...].astype(jnp.float32)
    if len(refs) > 4:
        wide_ref[row_count + MARGIN :] += refs[0][...].astype(jnp.float32)
    tall_ref[...] = grad_ref[...].astype(jnp.float32)
    sums_ref[...] = jnp.zeros_like(sums_ref)

    def some_rows(first, count, pairs):
        grads = [tall_ref[first - KERNEL + 1 + i].reshape(groups) if i in pairs else None
                 for i in range(count + KERNEL - 1)]
        for b in range(KERNEL):
            cells = [wide_ref[first + i, b : b + col_count, :].reshape(groups) for i in range(count)]
            for a in range(KERNEL):
                terms = [
                    grads[i - a + KERNEL - 1] * cells[i]
                    for i in range(count)
                    if i - a + KERNEL - 1 in pairs
                ]
                if terms:
                    sums_ref[a * KERNEL + b] += jnp.sum(sum(terms[1:], terms[0]), axis=0)

    def main_rows(step, carry):
        some_rows(KERNEL - 1 + 2 * step, 2, range(KERNEL + 1))
        return carry

    steps = (row_count - KERNEL + 1) // 2
    for first in range(0, KERNEL - 1, 2):
        some_rows(first, 2, range(KERNEL - 1 - first, KERNEL + 1))
    lax.fori_loop(0, steps, main_rows, 0)
    for first in range(KERNEL - 1 + 2 * steps, row_count + KERNEL - 1, 2):
        some_rows(first, 2, range(0, row_count + KERNEL - 1 - first))
    out_ref[...] = jnp.sum(sums_ref[...], axis=1)


def kernel_grad(grads, padded, mirror=None):
    rows, cols, channels = padded.shape
    row_count, col_count, _ = grads.shape
    operands = [grads, padded] + ([] if mirror is None else [mirror])
    return pl.pallas_call(
        kernel_grad_body,
        grid=(channels // LANES,),
        in_specs=[pl.BlockSpec((*part.shape[:2], LANES), lambda g: (0, 0, g)) for part in operands],
        out_specs=pl.BlockSpec((TAPS, LANES), lambda g: (0, g)),
        out_shape=jax.ShapeDtypeStruct((TAPS, channels), jnp.float32),
        scratch_shapes=[
            pltpu.VMEM((rows, cols, LANES), jnp.float32),
            pltpu.VMEM((row_count, col_count, LANES), jnp.float32),
            pltpu.VMEM((TAPS, 8, LANES), jnp.float32),
        ],
        cost_estimate=pl.CostEstimate(flops=10**9, bytes_accessed=3 << 20, transcendentals=0),
        compiler_params=pltpu.CompilerParams(vmem_limit_bytes=32 << 20),
        name="kernel_grad",
    )(*operands)


def add_last_rows(values, rows):
    return values + jnp.pad(rows, ((values.shape[0] - rows.shape[0], 0), (0, 0), (0, 0)))


def block_forward(
    padded, mixed_taps, mirror, start_field, kernel, norm_gain, inner_weight, outer_weight
):
    row_count, col_count, channels = start_field.shape
    if mirror is not None:
        mixed_taps = add_last_rows(mixed_taps, fold_taps(mirror, kernel, col_count))
    center = mixed_taps - jnp.mean(mixed_taps, axis=-1, keepdims=True)
    inverse = lax.rsqrt(jnp.mean(center * center, axis=-1, keepdims=True) + norm_eps)
    scaled = center * inverse
    normed = (scaled * norm_gain).astype(jnp.bfloat16).reshape(-1, channels)
    before = jnp.dot(normed, inner_weight, preferred_element_type=jnp.float32)
    hidden = (before * normal_cdf(before)).astype(jnp.bfloat16)
    branch = jnp.dot(hidden, outer_weight, preferred_element_type=jnp.float32).reshape(
        row_count, col_count, channels
    )
    return (branch, (padded, scaled, inverse, normed, before, hidden))


def block_backward(stored, norm_gain, inner_weight, outer_weight, incoming, together):
    _, scaled, inverse, normed, before, hidden = stored
    row_count, col_count, channels = scaled.shape
    rounded = incoming.astype(jnp.bfloat16).reshape(-1, channels)
    d_hidden = jnp.einsum("cd,fd->cf", rounded, outer_weight, preferred_element_type=jnp.float32)
    slopes = normal_cdf(before) + before * normal_density(before)
    d_before = (d_hidden * slopes).astype(jnp.bfloat16)
    sums = Sums(together, normed, d_before, hidden, rounded)
    sums.step()
    d_normed = jnp.einsum("cf,df->cd", d_before, inner_weight, preferred_element_type=jnp.float32)
    d_scaled = d_normed.reshape(row_count, col_count, channels) * norm_gain
    mean_grad = jnp.mean(d_scaled, axis=-1, keepdims=True)
    mean_cross = jnp.mean(d_scaled * scaled, axis=-1, keepdims=True)
    d_taps = (inverse * (d_scaled - mean_grad - scaled * mean_cross)).astype(jnp.bfloat16)
    return d_taps, sums


def in_column(tile):
    return lax.all_gather(tile, "narrow", axis=0, tiled=False)


def around(tile, reach):
    return beside_column(in_column(tile), reach)


def beside_column(column, reach):
    return [
        lax.ppermute(column, "wide", shift_pairs("wide", -offset, True)) if offset else column
        for offset in range(-reach, reach + 1)
    ]


def across(lhs, rhs):
    return lax.dot_general(lhs, rhs, (((1,), (1,)), ((), ())), preferred_element_type=jnp.float32)


def three_parts(values):
    parts = []
    for _ in range(3):
        part = values.astype(jnp.bfloat16)
        parts.append(part)
        values = values - part.astype(jnp.float32)
    return jnp.concatenate([part.astype(jnp.float32) for part in parts]).astype(jnp.bfloat16)


def summed(stacked):
    count = stacked.shape[0] // 3
    return stacked[:count] + stacked[count : 2 * count] + stacked[2 * count :]


def head_body(with_lists, state_ref, head_ref, *refs):
    out_ref = refs[-1]
    blocks = state_ref.shape[0] // LANES
    fields = head_ref.shape[0]
    rows = [
        across(head_ref[...], state_ref[pl.ds(block * LANES, LANES), :]) for block in range(blocks)
    ]
    if with_lists:
        for first in (0, 3):
            lists = [ref[0].astype(jnp.float32) for ref in refs[first : first + 3]]
            gap = jnp.zeros((1, LANES - lists[0].shape[1]), jnp.float32)
            sources, targets, weights = (jnp.concatenate([part, gap], axis=1) for part in lists)
            rows += [sources, targets, three_parts(weights).astype(jnp.float32)]
        rows.append(jnp.zeros((out_ref.shape[0] - blocks * fields - 10, LANES), jnp.float32))
    out_ref[...] = jnp.concatenate(rows).astype(jnp.bfloat16)


def coupled_fields(state, head_rows, lists=()):
    cells, channels = state.shape
    rows = cells // LANES * head_rows.shape[0] + (16 if lists else 0)
    operands = [state, head_rows, *lists]
    return pl.pallas_call(
        functools.partial(head_body, bool(lists)),
        out_shape=jax.ShapeDtypeStruct((rows, LANES), jnp.bfloat16),
        compiler_params=pltpu.CompilerParams(vmem_limit_bytes=32 << 20),
        name="coupled_fields",
    )(*operands)


def list_of(lists_ref, tile, which, first):
    rows = lists_ref[tile, first:, :].astype(jnp.float32)[5 * which : 5 * which + 5]
    return rows[0:1].astype(jnp.int32), rows[1:2].astype(jnp.int32), [rows[i : i + 1] for i in (2, 3, 4)]


def rows_like(index, parts, count):
    at = lax.broadcasted_iota(jnp.int32, (count, LANES), 0) == index
    return jnp.concatenate([jnp.where(at, part, 0.0) for part in parts]).astype(jnp.bfloat16)


def chosen(index):
    at = lax.broadcasted_iota(jnp.int32, (LANES, LANES), 0) == index
    return jnp.where(at, 1.0, 0.0).astype(jnp.bfloat16)


def remap_blocks(matrix, blocks_refs, cells_ref, sums_ref, fields, used):
    cells_ref[...] = jnp.zeros_like(cells_ref)
    lat_count = blocks_refs[0].shape[0]
    for i, ref in enumerate(blocks_refs):
        for tile in range(lat_count):
            cells_ref[pl.ds((i * lat_count + tile) * used, used), :] = ref[tile, :used, :].astype(jnp.float32)
    parts = three_parts(matrix)
    for k in range(fields):
        blocks = cells_ref[pl.ds(k, LANES, stride=fields), :].astype(jnp.bfloat16)
        mixed = jnp.dot(parts, blocks, preferred_element_type=jnp.float32)
        sums_ref[pl.ds(k, matrix.shape[0], stride=fields), :] = summed(mixed)


def lift_block(sums, weights):
    parts = three_parts(sums)
    return lax.dot_general(
        parts,
        jnp.concatenate([weights.astype(jnp.float32)] * 3).astype(jnp.bfloat16),
        (((0,), (0,)), ((), ())),
        preferred_element_type=jnp.float32,
    )


def start_body(which, masked, own_ref, *refs):
    lists, blocks = refs[:3], refs[3:8]
    state_ref, left_ref, right_ref, below_ref, above_ref, lift_ref, kernel_ref = refs[8:15]
    padded_ref, start_ref, taps_ref = refs[15:18]
    cells_ref, sums_ref, block_ref, wide_ref, spread_ref, wet_ref = refs[18:]
    lat_count = blocks[0].shape[0]
    row_count, col_count, _ = taps_ref.shape
    fields = lift_ref.shape[0]
    block_rows = LANES // col_count
    count = row_count // block_rows
    used = count * fields
    extra = block_rows - MARGIN
    own = own_ref[0]

    @pl.when(pl.program_id(0) == 0)
    def _():
        matrix = []
        for column in range(3):
            mixed = jnp.zeros((3 * (count + 2), LANES), jnp.float32)
            for beside in (-1, 0, 1):
                tile = own + beside
                inside = jnp.where((tile >= 0) & (tile < lat_count), 1.0, 0.0)
                sources, targets, parts = list_of(
                    lists[column], jnp.clip(tile, 0, lat_count - 1), which, used
                )
                placing = rows_like(
                    targets + 1 + beside * count, [part * inside for part in parts], count + 2
                )
                mixed = mixed + across(placing, chosen(sources + column * lat_count * count))
            matrix.append(summed(mixed))
        remap_blocks(jnp.concatenate(matrix), blocks, cells_ref, sums_ref, fields, used)

    wide_ref[...] = jnp.zeros_like(wide_ref)
    left, right = col_count + MARGIN, col_count + 2 * MARGIN
    rows = slice(extra, extra + row_count + 2 * MARGIN)
    inner = slice(extra + MARGIN, extra + MARGIN + row_count)
    top = slice(extra + MARGIN + row_count, extra + row_count + 2 * MARGIN)
    wide_ref[inner, 0:MARGIN, :] = left_ref[...].astype(jnp.float32)
    wide_ref[inner, MARGIN:left, :] = state_ref[...].astype(jnp.float32)
    wide_ref[inner, left:right, :] = right_ref[...].astype(jnp.float32)
    wide_ref[extra : extra + MARGIN, 0:right, :] = below_ref[...].astype(jnp.float32)
    wide_ref[top, 0:right, :] = above_ref[...].astype(jnp.float32)
    if masked:

        @pl.when(pl.program_id(0) == 0)
        def _():
            wet = jnp.where(wide_ref[rows, :, 0:1] < 100.0, 1.0, 0.0)
            wet_ref[...] = jnp.broadcast_to(wet, wet_ref.shape)

    for column in range(3):
        for block in range(count + 2):
            sums = sums_ref[pl.ds((column * (count + 2) + block) * fields, fields), :]
            block_ref[...] = lift_block(sums, lift_ref[...]).reshape(block_ref.shape)
            here = slice(block * block_rows, (block + 1) * block_rows)
            if column == 0:
                wide_ref[here, 0:MARGIN, :] += block_ref[:, col_count - MARGIN : col_count, :]
            elif column == 1:
                wide_ref[here, MARGIN:left, :] += block_ref[...]
            else:
                wide_ref[here, left:right, :] += block_ref[:, 0:MARGIN, :]
    start = wide_ref[rows]
    if masked:
        start = jnp.where(wet_ref[...] > 0.5, start, 0.0)
    start = start.astype(jnp.bfloat16)
    padded_ref[...] = start
    wide_ref[rows] = start.astype(jnp.float32)
    start_ref[...] = wide_ref[inner, MARGIN:left, :].astype(jnp.bfloat16)
    spread_taps(kernel_ref, spread_ref, False)
    convolve(wide_ref, extra, spread_ref, taps_ref)


def start_and_taps(which, masked, own, lists, blocks, states, lift_weight, kernel):
    row_count, col_count, channels = states[0].shape[1:]
    rows, cols = row_count + 2 * MARGIN, col_count + SIDE
    grid_index = 1 if masked else 0
    fields = lift_weight.shape[0]
    block_rows = LANES // col_count
    count = row_count // block_rows + 2
    whole = lambda part: pl.BlockSpec(part.shape, lambda g: (0, 0, 0))
    piece = lambda part: pl.BlockSpec((None, *part.shape[1:3], LANES), lambda g: (grid_index, 0, 0, g))
    return pl.pallas_call(
        functools.partial(start_body, which, masked),
        grid=(channels // LANES,),
        in_specs=[
            pl.BlockSpec(memory_space=pltpu.SMEM),
            *[whole(part) for part in lists],
            *[whole(part) for part in blocks],
            *[piece(part) for part in states],
            pl.BlockSpec((fields, LANES), lambda g: (0, g)),
            pl.BlockSpec((KERNEL, KERNEL, LANES), lambda g: (0, 0, g)),
        ],
        out_specs=[
            pl.BlockSpec((rows, cols, LANES), lambda g: (0, 0, g)),
            pl.BlockSpec((row_count, col_count, LANES), lambda g: (0, 0, g)),
            pl.BlockSpec((row_count, col_count, LANES), lambda g: (0, 0, g)),
        ],
        out_shape=[
            jax.ShapeDtypeStruct((rows, cols, channels), jnp.bfloat16),
            jax.ShapeDtypeStruct((row_count, col_count, channels), jnp.bfloat16),
            jax.ShapeDtypeStruct((row_count, col_count, channels), jnp.float32),
        ],
        scratch_shapes=[
            pltpu.VMEM((LANES * fields, LANES), jnp.float32),
            pltpu.VMEM((3 * count * fields, LANES), jnp.float32),
            pltpu.VMEM((block_rows, col_count, LANES), jnp.float32),
            pltpu.VMEM((count * block_rows, cols, LANES), jnp.float32),
            pltpu.VMEM((TAPS, 8, LANES), jnp.float32),
            pltpu.VMEM((rows, cols, LANES), jnp.float32),
        ],
        cost_estimate=pl.CostEstimate(flops=10**9, bytes_accessed=3 << 20, transcendentals=0),
        compiler_params=pltpu.CompilerParams(vmem_limit_bytes=56 << 20),
        name="start_and_taps",
    )(own, *lists, *blocks, *states, lift_weight, kernel)


def total_body(which, first, own_ref, *refs):
    lists, blocks = refs[:3], refs[3:6]
    head_ref, base_ref, out_ref, cells_ref, sums_ref = refs[6:]
    lat_count = blocks[0].shape[0]
    fields = head_ref.shape[0]
    count = base_ref.shape[0] // LANES
    own = own_ref[0]
    mixed = jnp.zeros((24, LANES), jnp.float32)
    for column in range(3):
        for tile in range(lat_count):
            sources, targets, parts = list_of(lists[column], tile, which, first)
            local = sources - ((2 - column) * lat_count + own) * count
            local = jnp.where(local < count, local, -1)
            place = chosen(targets + (column * lat_count + tile) * count)
            mixed = mixed + across(rows_like(local, parts, 8), place)
    remap_blocks(summed(mixed), blocks, cells_ref, sums_ref, fields, count * fields)
    for block in range(count):
        rows = pl.ds(block * LANES, LANES)
        back = lift_block(sums_ref[pl.ds(block * fields, fields), :], head_ref[...])
        out_ref[rows, :] = (base_ref[rows, :].astype(jnp.float32) + back).astype(out_ref.dtype)


def add_remap_adjoint(which, own, lists, blocks, head_rows, base, kind):
    fields = head_rows.shape[0]
    first = base.shape[0] // LANES * fields
    memory = pl.BlockSpec(memory_space=pltpu.VMEM)
    return pl.pallas_call(
        functools.partial(total_body, which, first),
        in_specs=[pl.BlockSpec(memory_space=pltpu.SMEM)] + [memory] * 8,
        out_shape=jax.ShapeDtypeStruct(base.shape, kind),
        scratch_shapes=[
            pltpu.VMEM((LANES * fields, LANES), jnp.float32),
            pltpu.VMEM((8 * fields, LANES), jnp.float32),
        ],
        compiler_params=pltpu.CompilerParams(vmem_limit_bytes=32 << 20),
        name="add_remap_adjoint",
    )(own, *lists, *blocks, head_rows, base)


def side_strips(states):
    size = states.shape[2]
    return (
        lax.ppermute(states[:, :, size - MARGIN :], "wide", shift_pairs("wide", 1, True)),
        lax.ppermute(states[:, :, :MARGIN], "wide", shift_pairs("wide", -1, True)),
    )


def end_strips(states, left, right):
    def across_columns(rows):
        return jnp.concatenate([left[:, rows], states[:, rows], right[:, rows]], axis=2)

    size = states.shape[1]
    return (
        lax.ppermute(across_columns(slice(size - MARGIN, size)), "narrow", shift_pairs("narrow", 1, False)),
        lax.ppermute(across_columns(slice(0, MARGIN)), "narrow", shift_pairs("narrow", -1, False)),
    )


def lift_back(gradient, lift_weight):
    return jnp.einsum(
        "bpd,kd->bkp",
        gradient.reshape(-1, 128, lift_weight.shape[1]),
        lift_weight.astype(jnp.float32),
        precision=highest,
    )


def per_device(
    atmos_state,
    ocean_state,
    wet_mask,
    atmos_kernel,
    atmos_gain,
    atmos_inner,
    atmos_outer,
    ocean_kernel,
    ocean_gain,
    ocean_inner,
    ocean_outer,
    flux_head,
    flux_lift,
    surface_head,
    surface_lift,
    flux_source,
    flux_target,
    flux_weight,
    surface_source,
    surface_target,
    surface_weight,
    atmos_cotangent,
    ocean_cotangent,
):
    row_count, col_count, channels = atmos_state.shape
    wet_cells = wet_mask.astype(jnp.float32)[:, :, None]
    own = lax.axis_index("narrow").reshape(1).astype(jnp.int32)
    lists = [flux_source, flux_target, flux_weight, surface_source, surface_target, surface_weight]
    flux_rows, surface_rows = flux_head.T, surface_head.T
    cells = row_count * col_count
    marked = jnp.where(wet_mask[:, :, None] > 0, ocean_state, jnp.bfloat16(1024.0))
    states = jnp.stack([atmos_state, marked])
    left, right = side_strips(states)
    column = in_column(coupled_fields(ocean_state.reshape(cells, channels), surface_rows, lists))
    column, left, right = lax.optimization_barrier((column, left, right))
    states = (states, left, right, *end_strips(states, left, right))
    first = beside_column(column, 2)
    lists = first[1:4]
    atmos_padded, atmos_start, atmos_taps = start_and_taps(
        1, False, own, lists, first, states, surface_lift, atmos_kernel
    )
    atmos_branch, atmos_stored = block_forward(
        atmos_padded, atmos_taps, None, atmos_start, atmos_kernel, atmos_gain, atmos_inner, atmos_outer
    )
    atmos_next = (atmos_start + atmos_branch).astype(jnp.bfloat16)
    fluxes = around(coupled_fields(atmos_next.reshape(cells, channels), flux_rows), 2)
    ocean_padded, ocean_start, ocean_taps = start_and_taps(
        0, True, own, lists, fluxes, states, flux_lift, ocean_kernel
    )
    own_rows = slice(MARGIN, MARGIN + row_count)
    mirror = roomy(fold_band(ocean_padded[own_rows, : col_count + 2 * MARGIN]))
    ocean_branch, ocean_stored = block_forward(
        ocean_padded, ocean_taps, mirror, ocean_start, ocean_kernel, ocean_gain, ocean_inner, ocean_outer
    )
    ocean_next = ((ocean_start + ocean_branch) * wet_cells).astype(jnp.bfloat16)
    ocean_total = ocean_cotangent * wet_cells
    ocean_d_taps, ocean_sums = block_backward(
        ocean_stored, ocean_gain, ocean_inner, ocean_outer, ocean_total, True
    )
    ocean_kernel_part = kernel_grad(ocean_d_taps, ocean_stored[0], mirror)
    grad_padded, grad_mirror = extend(ocean_d_taps, True, ocean_kernel_part)
    spread = apply_kernel(roomy(grad_padded), ocean_kernel, row_count, col_count, True)
    fold_part = fold_taps(roomy(grad_mirror), ocean_kernel, col_count)
    spread = add_last_rows(spread, fold_part)
    ocean_start_grad = (ocean_total + spread) * wet_cells
    flux_grads = lift_back(ocean_start_grad, flux_lift).astype(jnp.bfloat16)
    flux_grads = around(flux_grads.reshape(-1, LANES), 1)
    flux_grads = ocean_sums.hold(*flux_grads)
    ocean_sums.step()
    atmos_total = add_remap_adjoint(
        0, own, lists, flux_grads, flux_rows, atmos_cotangent.reshape(cells, channels), jnp.float32
    ).reshape(row_count, col_count, channels)
    atmos_d_taps, atmos_sums = block_backward(
        atmos_stored, atmos_gain, atmos_inner, atmos_outer, atmos_total, False
    )
    atmos_d_taps = atmos_sums.hold(atmos_d_taps)
    atmos_sums.step()
    atmos_kernel_part = kernel_grad(atmos_d_taps, atmos_stored[0])
    grad_padded, _ = extend(atmos_d_taps, False, atmos_kernel_part)
    grad_padded = ocean_sums.hold(grad_padded)
    ocean_sums.step()
    spread = apply_kernel(roomy(grad_padded), atmos_kernel, row_count, col_count, True)
    atmos_start_grad = atmos_total + spread
    atmos_state_grad = atmos_start_grad.astype(jnp.bfloat16)
    surface_grads = lift_back(atmos_start_grad, surface_lift).astype(jnp.bfloat16)
    surface_grads = atmos_sums.hold(surface_grads)
    atmos_sums.step()
    surface_grads = around(surface_grads.reshape(-1, LANES), 1)
    surface_grads = ocean_sums.hold(*surface_grads)
    ocean_state_grad = add_remap_adjoint(
        1, own, lists, surface_grads, surface_rows, ocean_start_grad.reshape(cells, channels), jnp.bfloat16
    ).reshape(row_count, col_count, channels)
    ocean_sums, atmos_sums = ocean_sums.result(), atmos_sums.result()
    kernel_sums = doubling_sum(jnp.stack([atmos_kernel_part, ocean_kernel_part])) / grad_scale
    kernel_sums = kernel_sums.reshape(2, KERNEL, KERNEL, channels)
    return (
        atmos_next,
        ocean_next,
        atmos_state_grad,
        ocean_state_grad,
        atmos_sums[0],
        atmos_sums[1],
        kernel_sums[0],
        ocean_sums[0],
        ocean_sums[1],
        kernel_sums[1],
    )


def solution(mesh):
    return jax.shard_map(
        per_device,
        mesh=mesh,
        in_specs=(
            P("narrow", "wide", None),
            P("narrow", "wide", None),
            P("narrow", "wide"),
            P(),
            P(),
            P(),
            P(),
            P(),
            P(),
            P(),
            P(),
            P(),
            P(),
            P(),
            P(),
            P("narrow", "wide", None),
            P("narrow", "wide", None),
            P("narrow", "wide", None),
            P("narrow", "wide", None),
            P("narrow", "wide", None),
            P("narrow", "wide", None),
            P("narrow", "wide", None),
            P("narrow", "wide", None),
        ),
        out_specs=(
            P("narrow", "wide", None),
            P("narrow", "wide", None),
            P("narrow", "wide", None),
            P("narrow", "wide", None),
            P(("wide", "narrow"), None),
            P(("wide", "narrow"), None),
            P(),
            P(("wide", "narrow"), None),
            P(("wide", "narrow"), None),
            P(),
        ),
        check_vma=False,
    )
```
